32 devices in a mesh: px: 4 (over y, x), py: 8 (over z, core).
Axes of the slice: x: 2, y: 2, z: 4, core: 2. Of those that a mesh axis runs over, the one named last changes fastest.
Arguments:
- carried: bfloat16 [2, 512, 512, 128], P(None, 'px', 'py'), may hold values from -0.59765625 to 0.59765625
- velocity: bfloat16 [2, 128, 128], P(None, ('px', 'py')), may hold values from -4 to 4
- strip_column: int32 [128], P(('px', 'py')), may hold values from 0 to 262143, as said below
- thick: float32 [128], replicated, may hold values from 0.5 to 2
Outputs:
- pressure: bfloat16 [2, 512, 512, 128], P(None, 'px', 'py')
- added_mass: float32 [2, 2], replicated
The draws below stay inside these ranges and needn't reach their ends.
Inputs may be any that keep to these rules, and one draw needn't show every extreme that they name: `strip_column`: no two strips share a grid column.
All inputs are finite; a program needn't handle non-finite values.
Results may differ from the reference program's by a relative error of at most 0.0081.
Values may be sent and summed in bfloat16 or wider, within the bound.
No kernel may reach another device: no remote copies, remote signals or barrier semaphores. Data moves between devices by JAX's collectives and lax.ppermute only.
A program may use at most 128 MiB of HBM per device.

```python
import math
import jax
import jax.numpy as jnp
from jax import lax

NX = 512
NY = 512
NZ = 128
MODES = 2
STRIPS = 128


def draw_strip_column(key, part):
    key = jax.random.fold_in(key, 5)
    return jax.random.permutation(key, NX * NY)[:STRIPS].astype(jnp.int32)


def draw_velocity(key, part):
    key = jax.random.fold_in(key, 11)
    key_shared, key_own, key_weight = jax.random.split(key, 3)
    weight = jax.random.uniform(key_weight, (MODES, 1, 1), jnp.float32, 0.6, 1.2)
    shared = jax.random.normal(key_shared, (1, STRIPS, NZ), jnp.float32)
    own = jax.random.normal(key_own, (MODES, STRIPS, NZ), jnp.float32)
    value = weight * shared + 0.6 * own
    return jnp.clip(value, -4.0, 4.0).astype(jnp.bfloat16)


def levels(own_key, extent, pieces, low, top_value):
    factor_of = 1.0
    for axis_at, blocks in pieces:
        heights = jax.random.uniform(jax.random.fold_in(jax.random.fold_in(own_key, 6), axis_at), (blocks,), jnp.float32, low / len(pieces), top_value / len(pieces))
        factor_of = factor_of * jnp.repeat(jnp.exp(heights), extent[axis_at] // blocks).reshape((-1,) + (1,) * (len(extent) - 1 - axis_at))
    return factor_of


def noise(own_key, dims, scale, limit, cuts=(), held_as=jnp.bfloat16):
    array = scale * jax.random.normal(own_key, dims, jnp.float32)
    if cuts:
        array = array * levels(own_key, dims, cuts, -0.22, 0.18)
    return jnp.clip(array, -limit, limit).astype(held_as)


def setup_inputs(seed: int = 0) -> dict:
    key_of = jax.random.split(jax.random.key(seed), 5)
    carried = noise(key_of[0], (MODES, NX, NY, NZ), 0.1, 0.59765625, ((1, 4), (2, 8)))
    velocity = draw_velocity(jax.random.fold_in(key_of[4], 71), 0)
    strip_column = draw_strip_column(jax.random.fold_in(key_of[4], 71), 0)
    thick = jnp.clip(jnp.exp(jax.random.uniform(key_of[3], (NZ,), jnp.float32, math.log(0.5), math.log(2.0))), 0.5, 2.0)
    return {"carried": carried, "velocity": velocity, "strip_column": strip_column, "thick": thick}


def sine_table(length):
    steps = jnp.arange(length, dtype=jnp.int32) + 1
    product = steps[:, None] * steps[None, :] % (2 * (length + 1))
    angle = product.astype(jnp.float32) * (math.pi / (length + 1))
    return (math.sqrt(2.0 / (length + 1)) * jnp.sin(angle)).astype(jnp.bfloat16)

def wave_numbers(position, length):
    return 2.0 - 2.0 * jnp.cos(math.pi * (position.astype(jnp.float32) + 1.0) / (length + 1))

def vertical_bands(thick):
    inv_gap = 2.0 / (thick[:-1] + thick[1:])
    nothing = jnp.zeros((1,), jnp.float32)
    sub_diag = -jnp.concatenate([nothing, inv_gap])
    super_diag = -jnp.concatenate([inv_gap, nothing])
    surface = jnp.concatenate([jnp.zeros((thick.shape[0] - 1,), jnp.float32), 2.0 / thick[-1:]])
    return (sub_diag, super_diag, surface - sub_diag - super_diag)

def shift_next(values, fill_value):
    return jnp.concatenate([values[..., 1:], jnp.full_like(values[..., :1], fill_value)], axis=-1)

def shift_prev(values):
    return jnp.concatenate([jnp.zeros_like(values[..., :1]), values[..., :-1]], axis=-1)

def reduce_solve(sub_diag, main_diag, super_diag, right_side):
    length = right_side.shape[-1]
    if length == 1:
        return right_side / main_diag
    sub_even, sub_odd = (sub_diag[..., 0::2], sub_diag[..., 1::2])
    main_even, main_odd = (main_diag[..., 0::2], main_diag[..., 1::2])
    super_even, super_odd = (super_diag[..., 0::2], super_diag[..., 1::2])
    right_even, right_odd = (right_side[..., 0::2], right_side[..., 1::2])
    alpha_left = -sub_odd / main_even
    gamma_right = -super_odd / shift_next(main_even, 1.0)
    new_sub = alpha_left * sub_even
    new_main = main_odd + alpha_left * super_even + gamma_right * shift_next(sub_even, 0.0)
    new_super = gamma_right * shift_next(super_even, 0.0)
    new_right = right_odd + alpha_left * right_even + gamma_right * shift_next(right_even, 0.0)
    odd_values = reduce_solve(new_sub, new_main, new_super, new_right)
    even_values = (right_even - sub_even * shift_prev(odd_values) - super_even * odd_values) / main_even
    joined = jnp.stack([even_values, odd_values], axis=-1)
    return joined.reshape(joined.shape[:-2] + (length,))

def reference(carried, velocity, strip_column, thick):
    modes_here = carried.shape[0]
    flat_grid = carried.astype(jnp.float32).reshape(modes_here, NX * NY, NZ)
    flat_grid = flat_grid.at[:, strip_column, :].add(velocity.astype(jnp.float32))
    source = flat_grid.reshape(modes_here, NX, NY, NZ).astype(jnp.bfloat16)
    sine_x = sine_table(NX).astype(jnp.float32)
    sine_y = sine_table(NY).astype(jnp.float32)
    wave_x = wave_numbers(jnp.arange(NX, dtype=jnp.int32), NX)
    wave_y = wave_numbers(jnp.arange(NY, dtype=jnp.int32), NY)
    sub_diag, super_diag, base_diag = vertical_bands(thick)
    block = math.gcd(NX, 128)
    highest = lax.Precision.HIGHEST

    def solve_block(inputs):
        spectrum_block, wave_block = inputs
        main_diag = base_diag + (wave_block[:, None, None] + wave_y[None, :, None]) * thick
        return reduce_solve(sub_diag, main_diag, super_diag, spectrum_block * thick)

    def one_mode(grid_field):
        row_spectrum = jnp.einsum('xyz,by->xbz', grid_field.astype(jnp.float32), sine_y, precision=highest).astype(jnp.bfloat16)
        spectrum = jnp.einsum('xbz,ax->abz', row_spectrum.astype(jnp.float32), sine_x, precision=highest)
        solved = lax.map(solve_block, (spectrum.reshape(NX // block, block, NY, NZ), wave_x.reshape(NX // block, block)))
        solved = solved.reshape(NX, NY, NZ).astype(jnp.bfloat16)
        row_pressure = jnp.einsum('abz,xa->xbz', solved.astype(jnp.float32), sine_x, precision=highest).astype(jnp.bfloat16)
        return jnp.einsum('xbz,yb->xyz', row_pressure.astype(jnp.float32), sine_y, precision=highest).astype(jnp.bfloat16)
    pressure = lax.map(one_mode, source)
    at_panels = pressure.reshape(modes_here, NX * NY, NZ)[:, strip_column, :].astype(jnp.float32)
    added_mass = jnp.einsum('isz,jsz,z->ij', at_panels, velocity.astype(jnp.float32), thick, precision=highest)
    return (pressure, added_mass / (STRIPS * NZ))
```

```python
import functools
import math

import jax
import jax.numpy as jnp
import ml_dtypes
import numpy as np
from jax import lax
from jax.experimental import pallas as pl
from jax.experimental.pallas import tpu as pltpu
from jax.sharding import PartitionSpec as P

VMEM_LIMIT = 56 * 1024 * 1024
VMEM = pltpu.MemorySpace.VMEM
SMEM = pltpu.MemorySpace.SMEM
LANES = 128


def sine_table(length):
    steps = np.arange(1, length + 1)
    product = steps[:, None] * steps[None, :] % (2 * (length + 1))
    return math.sqrt(2.0 / (length + 1)) * np.sin(product * (math.pi / (length + 1)))


def wave_numbers(length):
    return 4.0 * np.sin(np.arange(1, length + 1) * (math.pi / (2 * (length + 1)))) ** 2


def bf16(table):
    return jnp.asarray(table.astype(ml_dtypes.bfloat16))


def contract(left, right, left_dim, right_dim):
    return lax.dot_general(
        left, right, (((left_dim,), (right_dim,)), ((), ())), preferred_element_type=jnp.float32
    )


def forward_y_kernel(table_ref, grid_ref, out_ref, scratch):
    _, x_chunk, rows, layers = grid_ref.shape
    count, part = out_ref.shape[:2]
    group = table_ref.shape[0] // rows
    for start in range(0, x_chunk, group):
        block = grid_ref[0, start : start + group].reshape(group * rows, layers)
        result = contract(table_ref[...], block, 1, 0)
        for at in range(group):
            scratch[pl.ds(start + at, rows, stride=x_chunk), :] = result[
                at * rows : (at + 1) * rows
            ]
    out_ref[:, :, 0] = scratch[...].reshape(count, part, x_chunk, layers).astype(jnp.bfloat16)


def inverse_y_kernel(table_ref, in_ref, out_ref, scratch):
    _, x_chunk, rows, layers = out_ref.shape
    group = table_ref.shape[0] // rows
    scratch[...] = in_ref[:, :, 0].astype(jnp.float32).reshape(rows * x_chunk, layers)
    for start in range(0, x_chunk, group):
        block = jnp.concatenate(
            [scratch[pl.ds(start + at, rows, stride=x_chunk), :] for at in range(group)], axis=0
        ).astype(jnp.bfloat16)
        result = contract(table_ref[...], block, 1, 0)
        out_ref[0, start : start + group] = result.reshape(group, rows, layers).astype(
            jnp.bfloat16
        )


def y_table(rows):
    group = max(1, 256 // rows)
    return bf16(np.kron(np.eye(group), sine_table(rows)))


def forward_y(carried, count):
    modes, x_local, rows, layers = carried.shape
    chunk = 16
    part = rows // count
    table = y_table(rows)
    return pl.pallas_call(
        forward_y_kernel,
        grid=(modes, x_local // chunk),
        in_specs=[
            pl.BlockSpec(table.shape, lambda m, i: (0, 0)),
            pl.BlockSpec((1, chunk, rows, layers), lambda m, i: (m, i, 0, 0)),
        ],
        out_specs=pl.BlockSpec((count, part, 1, chunk, layers), lambda m, i: (0, 0, m, i, 0)),
        out_shape=jax.ShapeDtypeStruct((count, part, modes, x_local, layers), jnp.bfloat16),
        scratch_shapes=[pltpu.VMEM((rows * chunk, layers), jnp.float32)],
        compiler_params=pltpu.CompilerParams(vmem_limit_bytes=VMEM_LIMIT),
        name="forward_y",
    )(table, carried)


def inverse_y(spectra, rows):
    count, part, modes, x_local, layers = spectra.shape
    chunk = 16
    table = y_table(rows)
    return pl.pallas_call(
        inverse_y_kernel,
        grid=(modes, x_local // chunk),
        in_specs=[
            pl.BlockSpec(table.shape, lambda m, i: (0, 0)),
            pl.BlockSpec((count, part, 1, chunk, layers), lambda m, i: (0, 0, m, i, 0)),
        ],
        out_specs=pl.BlockSpec((1, chunk, rows, layers), lambda m, i: (m, i, 0, 0)),
        out_shape=jax.ShapeDtypeStruct((modes, x_local, rows, layers), jnp.bfloat16),
        scratch_shapes=[pltpu.VMEM((rows * chunk, layers), jnp.float32)],
        compiler_params=pltpu.CompilerParams(vmem_limit_bytes=VMEM_LIMIT),
        name="inverse_y",
    )(table, spectra)


def eliminate(thick_ref, gap_ref, wave_ref, modes, right_side, lower_ref, half_ref):
    layers = thick_ref.shape[0]
    group = wave_ref.shape[1]
    nothing = jnp.zeros(wave_ref.shape, jnp.float32)

    def step(k, carry):
        excess, sums = carry
        thick, inv_gap = thick_ref[k], gap_ref[k]
        spare = wave_ref[...] * thick + excess
        inverse = 1.0 / (spare + inv_gap)
        lower = inverse * inv_gap
        rows = pl.ds(pl.multiple_of(k * group, group), group)
        lower_ref[:, rows, :] = lower
        following = []
        for mode in range(modes):
            total = right_side(mode, k, rows) * thick + sums[mode]
            half_ref[mode, :, rows, :] = total * inverse
            following.append(total * lower)
        return (lower * spare, tuple(following))

    lax.fori_loop(0, layers, step, (nothing, (nothing,) * modes))


def substitute(layers, modes, lower_ref, half_ref, use):
    tiles, all_rows, lanes = lower_ref.shape
    group = all_rows // layers
    nothing = jnp.zeros((tiles, group, lanes), jnp.float32)

    def step(back, values):
        k = layers - 1 - back
        rows = pl.ds(pl.multiple_of(k * group, group), group)
        lower = lower_ref[:, rows, :]
        found = []
        for mode in range(modes):
            value = half_ref[mode, :, rows, :] + lower * values[mode]
            use(mode, k, rows, value)
            found.append(value)
        return tuple(found)

    lax.fori_loop(0, layers, step, (nothing,) * modes)


def put_rows(ref, mode, start, group, result):
    layers = result.shape[0]
    for tile in range(ref.shape[1]):
        ref[mode, tile, pl.ds(start, layers, stride=group), :] = result[
            :, tile * LANES : (tile + 1) * LANES
        ]


def take_rows(ref, mode, start, group, layers):
    return jnp.concatenate(
        [
            ref[mode, tile, pl.ds(start, layers, stride=group), :].astype(jnp.bfloat16)
            for tile in range(ref.shape[1])
        ],
        axis=1,
    )


def block_ends_kernel(
    thick_ref, gap_ref, wave_ref, ends_ref, table_ref, rows_ref, strips_ref,
    spectrum_ref, out_ref, lower_ref, half_ref, end_ref,
):
    count, part, modes, _, layers = rows_ref.shape
    tiles, group, _ = wave_ref.shape
    if group > part:
        spectrum_ref[...] = jnp.zeros_like(spectrum_ref)

    def transform(b, carry):
        for mode in range(modes):
            left = jnp.concatenate(
                [rows_ref[c, b, mode] for c in range(count)] + [strips_ref[b, mode]], axis=0
            )
            put_rows(spectrum_ref, mode, b, group, contract(left, table_ref[...], 0, 0))
        return carry

    lax.fori_loop(0, part, transform, 0)
    eliminate(
        thick_ref, gap_ref, wave_ref, modes,
        lambda mode, k, rows: spectrum_ref[mode, :, rows, :], lower_ref, half_ref,
    )

    def use(mode, k, rows, value):
        for end in range(2):
            end_ref[end * modes + mode, :, pl.ds(k, 1), :] = jnp.sum(
                value * ends_ref[end], axis=1, keepdims=True
            )

    substitute(layers, modes, lower_ref, half_ref, use)
    for at in range(2 * modes):
        for tile in range(tiles):
            out_ref[tile * LANES : (tile + 1) * LANES, at * layers : (at + 1) * layers] = (
                end_ref[at, tile].T.astype(jnp.bfloat16)
            )


def interface_kernel(
    thick_ref, gap_ref, wave_ref, spread_ref, in_ref,
    out_ref, sum_ref, next_ref, spectrum_ref, lower_ref, half_ref,
):
    group = wave_ref.shape[1]
    layers = thick_ref.shape[0]
    blocks = spread_ref.shape[0] // 2
    modes = in_ref.shape[2] // (2 * layers)
    here = in_ref.shape[1] // blocks
    if group > here:
        spectrum_ref[...] = jnp.zeros_like(spectrum_ref)
    total = jnp.sum(in_ref[...].astype(jnp.float32), axis=0)
    for at in range(2 * modes):
        sum_ref[at] = total[:, at * layers : (at + 1) * layers]

    for a in range(here):
        picked = pl.ds(a, blocks, stride=here)
        for mode in range(modes):
            left = jnp.concatenate(
                [sum_ref[end * modes + mode, picked, :] for end in range(2)], axis=0
            ).astype(jnp.bfloat16)
            put_rows(spectrum_ref, mode, a, group, contract(left, spread_ref[...], 0, 0))
    eliminate(
        thick_ref, gap_ref, wave_ref, modes,
        lambda mode, k, rows: spectrum_ref[mode, :, rows, :], lower_ref, half_ref,
    )

    def use(mode, k, rows, value):
        half_ref[mode, :, rows, :] = value

    substitute(layers, modes, lower_ref, half_ref, use)
    for a in range(here):
        picked = pl.ds(a, blocks, stride=here)
        for mode in range(modes):
            solved = take_rows(half_ref, mode, a, group, layers)
            found = contract(spread_ref[...], solved, 1, 1)
            for end in range(2):
                next_ref[end * modes + mode, picked, :] = found[
                    end * blocks : (end + 1) * blocks
                ]
    inner = (blocks - 1) * here
    for mode in range(modes):
        first, last = mode, modes + mode
        next_ref[first, here:] = next_ref[first, here:] + sum_ref[last, :inner]
        next_ref[last, :inner] = next_ref[last, :inner] + sum_ref[first, here:]
    for copy in range(out_ref.shape[0]):
        for at in range(2 * modes):
            out_ref[copy, :, at * layers : (at + 1) * layers] = next_ref[at].astype(
                jnp.bfloat16
            )


def block_solve_kernel(
    thick_ref, gap_ref, wave_ref, ends_ref, table_ref, spectrum_ref, bound_ref, strips_ref,
    out_ref, mass_ref, lower_ref, half_ref, edge_ref,
):
    count, part, modes, x_local, layers = out_ref.shape
    tiles, group, _ = wave_ref.shape
    for at in range(2 * modes):
        for tile in range(tiles):
            edge_ref[at, tile] = (
                bound_ref[tile * LANES : (tile + 1) * LANES, at * layers : (at + 1) * layers]
                .astype(jnp.float32)
                .T
            )

    def right_side(mode, k, rows):
        total = spectrum_ref[mode, :, rows, :]
        for end in range(2):
            total = total + ends_ref[end] * edge_ref[end * modes + mode, :, pl.ds(k, 1), :]
        return total

    eliminate(thick_ref, gap_ref, wave_ref, modes, right_side, lower_ref, half_ref)

    def use(mode, k, rows, value):
        half_ref[mode, :, rows, :] = value

    substitute(layers, modes, lower_ref, half_ref, use)

    def transform(b, sums):
        found = []
        for mode in range(modes):
            solved = take_rows(half_ref, mode, b, group, layers)
            result = contract(table_ref[...], solved, 1, 1)
            for c in range(count):
                out_ref[c, b, mode] = result[c * x_local : (c + 1) * x_local].astype(
                    jnp.bfloat16
                )
            found.append(result[count * x_local :])
        weights = [strips_ref[b, mode].astype(jnp.float32) for mode in range(modes)]
        return tuple(
            sums[i * modes + j] + jnp.sum(found[i] * weights[j], axis=0, keepdims=True)
            for i in range(modes)
            for j in range(modes)
        )

    nothing = jnp.zeros((1, layers), jnp.float32)
    sums = lax.fori_loop(0, part, transform, (nothing,) * (modes * modes))
    for at in range(modes * modes):
        mass_ref[at : at + 1, :] = sums[at]


def shards(carried, velocity, strip_column, thick):
    modes, x_local, y_local, layers = carried.shape
    count_px = lax.axis_size("px")
    count_py = lax.axis_size("py")
    index_px = lax.axis_index("px")
    index_py = lax.axis_index("py")
    devices = count_px * count_py
    width_x = x_local * count_px
    width_y = y_local * count_py
    part = y_local // count_px
    group = -(-part // 8) * 8
    here = width_x // devices
    group_a = -(-here // 8) * 8
    strip_count = velocity.shape[1] * devices
    both = ("px", "py")

    code = jnp.stack([strip_column // 65536, strip_column // 256 % 256, strip_column % 256])
    code = jnp.pad(code.T, ((0, 0), (0, layers - 3))).astype(jnp.bfloat16)
    packed = jnp.concatenate([velocity, code[None]], axis=0).transpose(1, 0, 2)
    packed = jnp.broadcast_to(packed[None], (devices,) + packed.shape)
    gathered = lax.all_to_all(packed, both, split_axis=0, concat_axis=0, tiled=True)
    gathered = gathered.reshape(strip_count, modes + 1, layers)
    code = gathered[:, modes, :3].astype(jnp.int32)
    column = code[:, 0] * 65536 + code[:, 1] * 256 + code[:, 2]
    all_velocity = gathered[:, :modes].astype(jnp.float32)

    table_x = bf16(sine_table(width_x))
    table_y = jnp.asarray(sine_table(y_local).astype(np.float32))
    local_y = column % width_y - index_py * y_local
    inside = (local_y >= 0) & (local_y < y_local)
    factor = jnp.where(inside[:, None], table_y[jnp.clip(local_y, 0, y_local - 1)], 0.0)
    factor = lax.dynamic_slice_in_dim(factor, index_px * part, part, axis=1)
    strips = (factor.T[:, None, :, None] * all_velocity.transpose(1, 0, 2)[None]).astype(
        jnp.bfloat16
    )
    table_strips = jnp.concatenate([table_x, table_x[column // width_y]], axis=0)

    gap = jnp.concatenate([2.0 / (thick[:-1] + thick[1:]), 2.0 / thick[-1:]])
    wave_x = jnp.asarray(wave_numbers(width_x).astype(np.float32))
    wave_y = jnp.asarray(wave_numbers(width_y).astype(np.float32))
    wave_block = jnp.asarray(wave_numbers(y_local).astype(np.float32))
    wave_b = lax.dynamic_slice_in_dim(wave_block, index_px * part, part)
    wave_b = jnp.pad(wave_b, (0, group - part))[:, None] + wave_x.reshape(-1, 1, LANES)
    wave_a = lax.dynamic_slice_in_dim(wave_x, (index_px * count_py + index_py) * here, here)
    wave_a = jnp.pad(wave_a, (0, group_a - here))[:, None] + wave_y.reshape(-1, 1, LANES)
    ends = lax.dynamic_slice_in_dim(table_y[:, (0, y_local - 1)], index_px * part, part)
    ends = jnp.pad(ends.T, ((0, 0), (0, group - part)))[:, :, None]
    ends = jnp.broadcast_to(ends, (2, group, LANES))

    block_index = np.arange(count_py)
    full = sine_table(width_y)
    not_first = (block_index > 0)[:, None]
    not_last = (block_index < count_py - 1)[:, None]
    before = np.maximum(block_index * y_local - 1, 0)
    after = np.minimum((block_index + 1) * y_local, width_y - 1)
    spread = np.concatenate([full[before] * not_first, full[after] * not_last])

    params = pltpu.CompilerParams(vmem_limit_bytes=VMEM_LIMIT)
    vmem = pl.BlockSpec(memory_space=VMEM)
    smem = pl.BlockSpec(memory_space=SMEM)
    float32 = jnp.float32
    tiles_x, tiles_y = width_x // LANES, width_y // LANES

    spectra = forward_y(carried, count_px)
    rows = lax.all_to_all(spectra, "px", split_axis=0, concat_axis=0, tiled=True)
    spectrum, block_ends = pl.pallas_call(
        block_ends_kernel,
        in_specs=[smem, smem] + [vmem] * 5,
        out_specs=[vmem, vmem],
        out_shape=[
            jax.ShapeDtypeStruct((modes, tiles_x, layers * group, LANES), float32),
            jax.ShapeDtypeStruct((width_x, 2 * modes * layers), jnp.bfloat16),
        ],
        scratch_shapes=[
            pltpu.VMEM((tiles_x, layers * group, LANES), float32),
            pltpu.VMEM((modes, tiles_x, layers * group, LANES), float32),
            pltpu.VMEM((2 * modes, tiles_x, layers, LANES), float32),
        ],
        compiler_params=params,
        name="block_ends",
    )(thick, gap, wave_b, ends, table_strips, rows, strips)

    arrived = lax.all_to_all(block_ends, both, split_axis=0, concat_axis=0, tiled=True)
    outgoing = pl.pallas_call(
        interface_kernel,
        in_specs=[smem, smem] + [vmem] * 3,
        out_specs=vmem,
        out_shape=jax.ShapeDtypeStruct(
            (count_px, count_py * here, 2 * modes * layers), jnp.bfloat16
        ),
        scratch_shapes=[
            pltpu.VMEM((2 * modes, count_py * here, layers), float32),
            pltpu.VMEM((2 * modes, count_py * here, layers), float32),
            pltpu.VMEM((modes, tiles_y, layers * group_a, LANES), float32),
            pltpu.VMEM((tiles_y, layers * group_a, LANES), float32),
            pltpu.VMEM((modes, tiles_y, layers * group_a, LANES), float32),
        ],
        compiler_params=params,
        name="interface",
    )(
        thick, gap, wave_a, bf16(spread),
        arrived.reshape(count_px, count_py * here, 2 * modes * layers),
    )
    bounds = lax.all_to_all(
        outgoing.reshape(width_x, 2 * modes * layers), both, split_axis=0, concat_axis=0, tiled=True
    )

    returned, mass = pl.pallas_call(
        block_solve_kernel,
        in_specs=[smem, smem] + [vmem] * 6,
        out_specs=[vmem, vmem],
        out_shape=[
            jax.ShapeDtypeStruct((count_px, part, modes, x_local, layers), jnp.bfloat16),
            jax.ShapeDtypeStruct((modes * modes, layers), float32),
        ],
        scratch_shapes=[
            pltpu.VMEM((tiles_x, layers * group, LANES), float32),
            pltpu.VMEM((modes, tiles_x, layers * group, LANES), float32),
            pltpu.VMEM((2 * modes, tiles_x, layers, LANES), float32),
        ],
        compiler_params=params,
        name="block_solve",
    )(thick, gap, wave_b, ends, table_strips, spectrum, bounds, strips)
    back = lax.all_to_all(returned, "px", split_axis=0, concat_axis=0, tiled=True)
    pressure = inverse_y(back, y_local)
    local_mass = jnp.sum(mass * thick[None, :], axis=1).reshape(modes, modes)
    added_mass = lax.psum(local_mass, both) / (strip_count * layers)
    return (pressure, added_mass)


def solution(mesh):
    return jax.shard_map(
        shards,
        mesh=mesh,
        in_specs=(P(None, "px", "py", None), P(None, ("px", "py"), None), P(("px", "py")), P()),
        out_specs=(P(None, "px", "py", None), P()),
        check_vma=False,
    )
```

```python
import functools
import math

import jax
import jax.numpy as jnp
import ml_dtypes
import numpy as np
from jax import lax
from jax.experimental import pallas as pl
from jax.experimental.pallas import tpu as pltpu
from jax.sharding import PartitionSpec as P

VMEM_LIMIT = 36 * 1024 * 1024
VMEM = pltpu.MemorySpace.VMEM
SMEM = pltpu.MemorySpace.SMEM
LANES = 128


def sine_table(length):
    steps = np.arange(1, length + 1)
    product = steps[:, None] * steps[None, :] % (2 * (length + 1))
    return math.sqrt(2.0 / (length + 1)) * np.sin(product * (math.pi / (length + 1)))


def wave_numbers(length):
    return 4.0 * np.sin(np.arange(1, length + 1) * (math.pi / (2 * (length + 1)))) ** 2


def bf16(table):
    return jnp.asarray(table.astype(ml_dtypes.bfloat16))


def contract(left, right, left_dim, right_dim):
    return lax.dot_general(
        left, right, (((left_dim,), (right_dim,)), ((), ())), preferred_element_type=jnp.float32
    )


def forward_y_kernel(table_ref, grid_ref, out_ref, scratch):
    _, x_chunk, rows, layers = grid_ref.shape
    count, part = out_ref.shape[:2]
    group = table_ref.shape[0] // rows
    for start in range(0, x_chunk, group):
        block = grid_ref[0, start : start + group].reshape(group * rows, layers)
        result = contract(table_ref[...], block, 1, 0)
        for at in range(group):
            scratch[pl.ds(start + at, rows, stride=x_chunk), :] = result[
                at * rows : (at + 1) * rows
            ]
    out_ref[:, :, 0] = scratch[...].reshape(count, part, x_chunk, layers).astype(jnp.bfloat16)


def inverse_y_kernel(table_ref, in_ref, out_ref, scratch):
    _, x_chunk, rows, layers = out_ref.shape
    group = table_ref.shape[0] // rows
    scratch[...] = in_ref[:, :, 0].astype(jnp.float32).reshape(rows * x_chunk, layers)
    for start in range(0, x_chunk, group):
        block = jnp.concatenate(
            [scratch[pl.ds(start + at, rows, stride=x_chunk), :] for at in range(group)], axis=0
        ).astype(jnp.bfloat16)
        result = contract(table_ref[...], block, 1, 0)
        out_ref[0, start : start + group] = result.reshape(group, rows, layers).astype(
            jnp.bfloat16
        )


def y_table(rows):
    group = max(1, 256 // rows)
    return bf16(np.kron(np.eye(group), sine_table(rows)))


def forward_y(carried, count):
    modes, x_local, rows, layers = carried.shape
    chunk = 16
    part = rows // count
    table = y_table(rows)
    return pl.pallas_call(
        forward_y_kernel,
        grid=(modes, x_local // chunk),
        in_specs=[
            pl.BlockSpec(table.shape, lambda m, i: (0, 0)),
            pl.BlockSpec((1, chunk, rows, layers), lambda m, i: (m, i, 0, 0)),
        ],
        out_specs=pl.BlockSpec((count, part, 1, chunk, layers), lambda m, i: (0, 0, m, i, 0)),
        out_shape=jax.ShapeDtypeStruct((count, part, modes, x_local, layers), jnp.bfloat16),
        scratch_shapes=[pltpu.VMEM((rows * chunk, layers), jnp.float32)],
        compiler_params=pltpu.CompilerParams(vmem_limit_bytes=VMEM_LIMIT),
        name="forward_y",
    )(table, carried)


def inverse_y(spectra, rows):
    count, part, modes, x_local, layers = spectra.shape
    chunk = min(64, x_local)
    table = y_table(rows)
    return pl.pallas_call(
        inverse_y_kernel,
        grid=(modes, x_local // chunk),
        in_specs=[
            pl.BlockSpec(table.shape, lambda m, i: (0, 0)),
            pl.BlockSpec((count, part, 1, chunk, layers), lambda m, i: (0, 0, m, i, 0)),
        ],
        out_specs=pl.BlockSpec((1, chunk, rows, layers), lambda m, i: (m, i, 0, 0)),
        out_shape=jax.ShapeDtypeStruct((modes, x_local, rows, layers), jnp.bfloat16),
        scratch_shapes=[pltpu.VMEM((rows * chunk, layers), jnp.float32)],
        compiler_params=pltpu.CompilerParams(vmem_limit_bytes=VMEM_LIMIT),
        name="inverse_y",
    )(table, spectra)


def eliminate(thick_ref, gap_ref, wave_ref, modes, right_side, lower_ref, half_ref):
    layers = thick_ref.shape[0]
    group = wave_ref.shape[1]
    nothing = jnp.zeros(wave_ref.shape, jnp.float32)

    def step(k, carry):
        excess, sums = carry
        thick, inv_gap = thick_ref[k], gap_ref[k]
        spare = wave_ref[...] * thick + excess
        inverse = 1.0 / (spare + inv_gap)
        lower = inverse * inv_gap
        rows = pl.ds(pl.multiple_of(k * group, group), group)
        lower_ref[:, rows, :] = lower
        following = []
        for mode in range(modes):
            total = right_side(mode, k, rows) * thick + sums[mode]
            half_ref[mode, :, rows, :] = total * inverse
            following.append(total * lower)
        return (lower * spare, tuple(following))

    lax.fori_loop(0, layers, step, (nothing, (nothing,) * modes))


def substitute(layers, modes, lower_ref, half_ref, use):
    tiles, all_rows, lanes = lower_ref.shape
    group = all_rows // layers
    nothing = jnp.zeros((tiles, group, lanes), jnp.float32)

    def step(back, values):
        k = layers - 1 - back
        rows = pl.ds(pl.multiple_of(k * group, group), group)
        lower = lower_ref[:, rows, :]
        found = []
        for mode in range(modes):
            value = half_ref[mode, :, rows, :] + lower * values[mode]
            use(mode, k, rows, value)
            found.append(value)
        return tuple(found)

    lax.fori_loop(0, layers, step, (nothing,) * modes)


def put_rows(ref, mode, start, group, result):
    layers = result.shape[0]
    for tile in range(ref.shape[1]):
        ref[mode, tile, pl.ds(start, layers, stride=group), :] = result[
            :, tile * LANES : (tile + 1) * LANES
        ]


def take_rows(ref, mode, start, group, layers):
    return jnp.concatenate(
        [
            ref[mode, tile, pl.ds(start, layers, stride=group), :].astype(jnp.bfloat16)
            for tile in range(ref.shape[1])
        ],
        axis=1,
    )


def block_ends_kernel(
    thick_ref, gap_ref, wave_ref, ends_ref, table_ref, rows_ref, strips_ref,
    spectrum_ref, out_ref, lower_ref, half_ref, end_ref,
):
    count, part, modes, _, layers = rows_ref.shape
    tiles, group, _ = wave_ref.shape
    if group > part:
        spectrum_ref[...] = jnp.zeros_like(spectrum_ref)

    def transform(b, carry):
        for mode in range(modes):
            left = jnp.concatenate(
                [rows_ref[c, b, mode] for c in range(count)] + [strips_ref[b, mode]], axis=0
            )
            put_rows(spectrum_ref, mode, b, group, contract(left, table_ref[...], 0, 0))
        return carry

    lax.fori_loop(0, part, transform, 0)
    eliminate(
        thick_ref, gap_ref, wave_ref, modes,
        lambda mode, k, rows: spectrum_ref[mode, :, rows, :], lower_ref, half_ref,
    )

    def use(mode, k, rows, value):
        for end in range(2):
            end_ref[end * modes + mode, :, pl.ds(k, 1), :] = jnp.sum(
                value * ends_ref[end], axis=1, keepdims=True
            )

    substitute(layers, modes, lower_ref, half_ref, use)
    for at in range(2 * modes):
        for tile in range(tiles):
            out_ref[tile * LANES : (tile + 1) * LANES, at * layers : (at + 1) * layers] = (
                end_ref[at, tile].T.astype(jnp.bfloat16)
            )


def interface_kernel(
    thick_ref, gap_ref, wave_ref, spread_ref, in_ref,
    out_ref, sum_ref, next_ref, spectrum_ref, lower_ref, half_ref,
):
    group = wave_ref.shape[1]
    layers = thick_ref.shape[0]
    blocks = spread_ref.shape[0] // 2
    modes = in_ref.shape[2] // (2 * layers)
    here = in_ref.shape[1] // blocks
    if group > here:
        spectrum_ref[...] = jnp.zeros_like(spectrum_ref)
    total = jnp.sum(in_ref[...].astype(jnp.float32), axis=0)
    for at in range(2 * modes):
        sum_ref[at] = total[:, at * layers : (at + 1) * layers]

    for a in range(here):
        picked = pl.ds(a, blocks, stride=here)
        for mode in range(modes):
            left = jnp.concatenate(
                [sum_ref[end * modes + mode, picked, :] for end in range(2)], axis=0
            ).astype(jnp.bfloat16)
            put_rows(spectrum_ref, mode, a, group, contract(left, spread_ref[...], 0, 0))
    eliminate(
        thick_ref, gap_ref, wave_ref, modes,
        lambda mode, k, rows: spectrum_ref[mode, :, rows, :], lower_ref, half_ref,
    )

    def use(mode, k, rows, value):
        half_ref[mode, :, rows, :] = value

    substitute(layers, modes, lower_ref, half_ref, use)
    for a in range(here):
        picked = pl.ds(a, blocks, stride=here)
        for mode in range(modes):
            solved = take_rows(half_ref, mode, a, group, layers)
            found = contract(spread_ref[...], solved, 1, 1)
            for end in range(2):
                next_ref[end * modes + mode, picked, :] = found[
                    end * blocks : (end + 1) * blocks
                ]
    inner = (blocks - 1) * here
    for mode in range(modes):
        first, last = mode, modes + mode
        next_ref[first, here:] = next_ref[first, here:] + sum_ref[last, :inner]
        next_ref[last, :inner] = next_ref[last, :inner] + sum_ref[first, here:]
    for copy in range(out_ref.shape[0]):
        for at in range(2 * modes):
            out_ref[copy, :, at * layers : (at + 1) * layers] = next_ref[at].astype(
                jnp.bfloat16
            )


def block_solve_kernel(
    thick_ref, gap_ref, wave_ref, ends_ref, table_ref, spectrum_ref, bound_ref, strips_ref,
    out_ref, mass_ref, lower_ref, half_ref, edge_ref,
):
    count, part, modes, x_local, layers = out_ref.shape
    tiles, group, _ = wave_ref.shape
    for at in range(2 * modes):
        for tile in range(tiles):
            edge_ref[at, tile] = (
                bound_ref[tile * LANES : (tile + 1) * LANES, at * layers : (at + 1) * layers]
                .astype(jnp.float32)
                .T
            )

    def right_side(mode, k, rows):
        total = spectrum_ref[mode, :, rows, :]
        for end in range(2):
            total = total + ends_ref[end] * edge_ref[end * modes + mode, :, pl.ds(k, 1), :]
        return total

    eliminate(thick_ref, gap_ref, wave_ref, modes, right_side, lower_ref, half_ref)

    def use(mode, k, rows, value):
        half_ref[mode, :, rows, :] = value

    substitute(layers, modes, lower_ref, half_ref, use)

    def transform(b, sums):
        found = []
        for mode in range(modes):
            solved = take_rows(half_ref, mode, b, group, layers)
            result = contract(table_ref[...], solved, 1, 1)
            for c in range(count):
                out_ref[c, b, mode] = result[c * x_local : (c + 1) * x_local].astype(
                    jnp.bfloat16
                )
            found.append(result[count * x_local :])
        weights = [strips_ref[b, mode].astype(jnp.float32) for mode in range(modes)]
        return tuple(
            sums[i * modes + j] + jnp.sum(found[i] * weights[j], axis=0, keepdims=True)
            for i in range(modes)
            for j in range(modes)
        )

    nothing = jnp.zeros((1, layers), jnp.float32)
    sums = lax.fori_loop(0, part, transform, (nothing,) * (modes * modes))
    for at in range(modes * modes):
        mass_ref[at : at + 1, :] = sums[at]


def shards(carried, velocity, strip_column, thick):
    modes, x_local, y_local, layers = carried.shape
    count_px = lax.axis_size("px")
    count_py = lax.axis_size("py")
    index_px = lax.axis_index("px")
    index_py = lax.axis_index("py")
    devices = count_px * count_py
    width_x = x_local * count_px
    width_y = y_local * count_py
    part = y_local // count_px
    group = -(-part // 8) * 8
    here = width_x // devices
    group_a = -(-here // 8) * 8
    strip_count = velocity.shape[1] * devices
    both = ("px", "py")

    code = jnp.stack([strip_column // 65536, strip_column // 256 % 256, strip_column % 256])
    code = jnp.pad(code.T, ((0, 0), (0, layers - 3))).astype(jnp.bfloat16)
    packed = jnp.concatenate([velocity, code[None]], axis=0).transpose(1, 0, 2)
    packed = jnp.broadcast_to(packed[None], (devices,) + packed.shape)
    spectra, packed = lax.optimization_barrier((forward_y(carried, count_px), packed))
    gathered = lax.all_to_all(packed, both, split_axis=0, concat_axis=0, tiled=True)
    gathered = gathered.reshape(strip_count, modes + 1, layers)
    code = gathered[:, modes, :3].astype(jnp.int32)
    column = code[:, 0] * 65536 + code[:, 1] * 256 + code[:, 2]
    all_velocity = gathered[:, :modes].astype(jnp.float32)

    table_x = bf16(sine_table(width_x))
    table_y = jnp.asarray(sine_table(y_local).astype(np.float32))
    local_y = column % width_y - index_py * y_local
    inside = (local_y >= 0) & (local_y < y_local)
    factor = jnp.where(inside[:, None], table_y[jnp.clip(local_y, 0, y_local - 1)], 0.0)
    factor = lax.dynamic_slice_in_dim(factor, index_px * part, part, axis=1)
    strips = (factor.T[:, None, :, None] * all_velocity.transpose(1, 0, 2)[None]).astype(
        jnp.bfloat16
    )
    table_strips = jnp.concatenate([table_x, table_x[column // width_y]], axis=0)

    gap = jnp.concatenate([2.0 / (thick[:-1] + thick[1:]), 2.0 / thick[-1:]])
    wave_x = jnp.asarray(wave_numbers(width_x).astype(np.float32))
    wave_y = jnp.asarray(wave_numbers(width_y).astype(np.float32))
    wave_block = jnp.asarray(wave_numbers(y_local).astype(np.float32))
    wave_b = lax.dynamic_slice_in_dim(wave_block, index_px * part, part)
    wave_b = jnp.pad(wave_b, (0, group - part))[:, None] + wave_x.reshape(-1, 1, LANES)
    wave_a = lax.dynamic_slice_in_dim(wave_x, (index_px * count_py + index_py) * here, here)
    wave_a = jnp.pad(wave_a, (0, group_a - here))[:, None] + wave_y.reshape(-1, 1, LANES)
    ends = lax.dynamic_slice_in_dim(table_y[:, (0, y_local - 1)], index_px * part, part)
    ends = jnp.pad(ends.T, ((0, 0), (0, group - part)))[:, :, None]
    ends = jnp.broadcast_to(ends, (2, group, LANES))

    block_index = np.arange(count_py)
    full = sine_table(width_y)
    not_first = (block_index > 0)[:, None]
    not_last = (block_index < count_py - 1)[:, None]
    before = np.maximum(block_index * y_local - 1, 0)
    after = np.minimum((block_index + 1) * y_local, width_y - 1)
    spread = np.concatenate([full[before] * not_first, full[after] * not_last])

    params = pltpu.CompilerParams(vmem_limit_bytes=VMEM_LIMIT)
    vmem = pl.BlockSpec(memory_space=VMEM)
    smem = pl.BlockSpec(memory_space=SMEM)
    float32 = jnp.float32
    tiles_x, tiles_y = width_x // LANES, width_y // LANES

    rows = lax.all_to_all(spectra, "px", split_axis=0, concat_axis=0, tiled=True)
    spectrum, block_ends = pl.pallas_call(
        block_ends_kernel,
        in_specs=[smem, smem] + [vmem] * 5,
        out_specs=[vmem, vmem],
        out_shape=[
            jax.ShapeDtypeStruct((modes, tiles_x, layers * group, LANES), float32),
            jax.ShapeDtypeStruct((width_x, 2 * modes * layers), jnp.bfloat16),
        ],
        scratch_shapes=[
            pltpu.VMEM((tiles_x, layers * group, LANES), float32),
            pltpu.VMEM((modes, tiles_x, layers * group, LANES), float32),
            pltpu.VMEM((2 * modes, tiles_x, layers, LANES), float32),
        ],
        compiler_params=params,
        name="block_ends",
    )(thick, gap, wave_b, ends, table_strips, rows, strips)

    arrived = lax.all_to_all(block_ends, both, split_axis=0, concat_axis=0, tiled=True)
    outgoing = pl.pallas_call(
        interface_kernel,
        in_specs=[smem, smem] + [vmem] * 3,
        out_specs=vmem,
        out_shape=jax.ShapeDtypeStruct(
            (count_px, count_py * here, 2 * modes * layers), jnp.bfloat16
        ),
        scratch_shapes=[
            pltpu.VMEM((2 * modes, count_py * here, layers), float32),
            pltpu.VMEM((2 * modes, count_py * here, layers), float32),
            pltpu.VMEM((modes, tiles_y, layers * group_a, LANES), float32),
            pltpu.VMEM((tiles_y, layers * group_a, LANES), float32),
            pltpu.VMEM((modes, tiles_y, layers * group_a, LANES), float32),
        ],
        compiler_params=params,
        name="interface",
    )(
        thick, gap, wave_a, bf16(spread),
        arrived.reshape(count_px, count_py * here, 2 * modes * layers),
    )
    bounds = lax.all_to_all(
        outgoing.reshape(width_x, 2 * modes * layers), both, split_axis=0, concat_axis=0, tiled=True
    )

    returned, mass = pl.pallas_call(
        block_solve_kernel,
        in_specs=[smem, smem] + [vmem] * 6,
        out_specs=[vmem, vmem],
        out_shape=[
            jax.ShapeDtypeStruct((count_px, part, modes, x_local, layers), jnp.bfloat16),
            jax.ShapeDtypeStruct((modes * modes, layers), float32),
        ],
        scratch_shapes=[
            pltpu.VMEM((tiles_x, layers * group, LANES), float32),
            pltpu.VMEM((modes, tiles_x, layers * group, LANES), float32),
            pltpu.VMEM((2 * modes, tiles_x, layers, LANES), float32),
        ],
        compiler_params=params,
        name="block_solve",
    )(thick, gap, wave_b, ends, table_strips, spectrum, bounds, strips)
    back = lax.all_to_all(returned, "px", split_axis=0, concat_axis=0, tiled=True)
    pressure = inverse_y(back, y_local)
    local_mass = jnp.sum(mass * thick[None, :], axis=1).reshape(modes, modes)
    every_mass = jnp.broadcast_to(local_mass[None], (devices, modes, modes))
    every_mass = lax.all_to_all(every_mass, both, split_axis=0, concat_axis=0, tiled=True)
    added_mass = jnp.sum(every_mass, axis=0) / (strip_count * layers)
    return (pressure, added_mass)


def solution(mesh):
    return jax.shard_map(
        shards,
        mesh=mesh,
        in_specs=(P(None, "px", "py", None), P(None, ("px", "py"), None), P(("px", "py")), P()),
        out_specs=(P(None, "px", "py", None), P()),
        check_vma=False,
    )
```

```python
import functools
import math

import jax
import jax.numpy as jnp
import ml_dtypes
import numpy as np
from jax import lax
from jax.experimental import pallas as pl
from jax.experimental.pallas import tpu as pltpu
from jax.sharding import PartitionSpec as P

VMEM_LIMIT = 58 * 1024 * 1024
VMEM = pltpu.MemorySpace.VMEM
SMEM = pltpu.MemorySpace.SMEM
LANES = 128
CHUNK = 64


def sine_table(length):
    steps = np.arange(1, length + 1)
    product = steps[:, None] * steps[None, :] % (2 * (length + 1))
    return math.sqrt(2.0 / (length + 1)) * np.sin(product * (math.pi / (length + 1)))


def wave_numbers(length):
    return 4.0 * np.sin(np.arange(1, length + 1) * (math.pi / (2 * (length + 1)))) ** 2


def bf16(table):
    return jnp.asarray(table.astype(ml_dtypes.bfloat16))


def contract(left, right, left_dim, right_dim):
    return lax.dot_general(
        left, right, (((left_dim,), (right_dim,)), ((), ())), preferred_element_type=jnp.float32
    )


def pitch_of(group):
    return group if group // 8 % 2 else group + 8


def forward_y_kernel(table_ref, grid_ref, out_ref, scratch):
    _, x_chunk, rows, layers = grid_ref.shape
    pieces, part = out_ref.shape[:2]
    group = table_ref.shape[0] // rows
    for start in range(0, x_chunk, group):
        block = grid_ref[0, start : start + group].reshape(group * rows, layers)
        result = contract(table_ref[...], block, 1, 0)
        for at in range(group):
            scratch[pl.ds(start + at, rows, stride=pitch_of(x_chunk)), :] = result[
                at * rows : (at + 1) * rows
            ]
    for b in range(rows):
        begin = b * pitch_of(x_chunk)
        out_ref[b // part, b % part] = scratch[begin : begin + x_chunk, :].astype(jnp.bfloat16)


def inverse_y_kernel(table_ref, in_ref, out_ref, scratch):
    _, x_chunk, rows, layers = out_ref.shape
    group = table_ref.shape[0] // rows
    part = in_ref.shape[1]
    for b in range(rows):
        begin = b * pitch_of(x_chunk)
        scratch[begin : begin + x_chunk, :] = in_ref[b // part, b % part].astype(jnp.float32)
    for start in range(0, x_chunk, group):
        block = jnp.concatenate(
            [
                scratch[pl.ds(start + at, rows, stride=pitch_of(x_chunk)), :]
                for at in range(group)
            ],
            axis=0,
        ).astype(jnp.bfloat16)
        result = contract(table_ref[...], block, 1, 0)
        out_ref[0, start : start + group] = result.reshape(group, rows, layers).astype(
            jnp.bfloat16
        )


def y_table(rows):
    group = max(1, 256 // rows)
    return bf16(np.kron(np.eye(group), sine_table(rows)))


def forward_y(carried, count):
    modes, x_local, rows, layers = carried.shape
    chunk = min(CHUNK, x_local)
    pieces = count // modes
    part = rows // pieces
    table = y_table(rows)
    return pl.pallas_call(
        forward_y_kernel,
        grid=(modes, x_local // chunk),
        in_specs=[
            pl.BlockSpec(table.shape, lambda m, i: (0, 0)),
            pl.BlockSpec((1, chunk, rows, layers), lambda m, i: (m, i, 0, 0)),
        ],
        out_specs=pl.BlockSpec((pieces, part, chunk, layers), lambda m, i: (m, 0, i, 0)),
        out_shape=jax.ShapeDtypeStruct((count, part, x_local, layers), jnp.bfloat16),
        scratch_shapes=[pltpu.VMEM((rows * pitch_of(chunk), layers), jnp.float32)],
        compiler_params=pltpu.CompilerParams(vmem_limit_bytes=VMEM_LIMIT),
        name="forward_y",
    )(table, carried)


def inverse_y(spectra, rows):
    count, part, x_local, layers = spectra.shape
    pieces = rows // part
    modes = count // pieces
    chunk = min(CHUNK, x_local)
    table = y_table(rows)
    return pl.pallas_call(
        inverse_y_kernel,
        grid=(modes, x_local // chunk),
        in_specs=[
            pl.BlockSpec(table.shape, lambda m, i: (0, 0)),
            pl.BlockSpec((pieces, part, chunk, layers), lambda m, i: (m, 0, i, 0)),
        ],
        out_specs=pl.BlockSpec((1, chunk, rows, layers), lambda m, i: (m, i, 0, 0)),
        out_shape=jax.ShapeDtypeStruct((modes, x_local, rows, layers), jnp.bfloat16),
        scratch_shapes=[pltpu.VMEM((rows * pitch_of(chunk), layers), jnp.float32)],
        compiler_params=pltpu.CompilerParams(vmem_limit_bytes=VMEM_LIMIT),
        name="inverse_y",
    )(table, spectra)


def at_layer(k, group, pitch):
    return pl.ds(pl.multiple_of(k * pitch, 8), group)


def eliminate(
    thick_ref, gap_ref, wave_ref, modes, right_side, lower_ref, half_ref, ready=(None,)
):
    layers = thick_ref.shape[0]
    group = wave_ref.shape[1]
    nothing = jnp.zeros(wave_ref.shape, jnp.float32)

    def step(k, carry):
        excess, sums = carry
        thick, inv_gap = thick_ref[k], gap_ref[k]
        spare = wave_ref[...] * thick + excess
        inverse = 1.0 / (spare + inv_gap)
        lower = inverse * inv_gap
        rows = at_layer(k, group, pitch_of(group))
        lower_ref[:, at_layer(k, group, group), :] = lower
        following = []
        for mode in range(modes):
            total = right_side(mode, k, rows) * thick + sums[mode]
            half_ref[mode, :, rows, :] = total * inverse
            following.append(total * lower)
        return (lower * spare, tuple(following))

    carry = (nothing, (nothing,) * modes)
    each = layers // len(ready)
    for at, wait in enumerate(ready):
        if wait is not None:
            wait()
        carry = lax.fori_loop(at * each, (at + 1) * each, step, carry)


def substitute(layers, modes, lower_ref, half_ref, use):
    tiles, all_rows, lanes = lower_ref.shape
    group = all_rows // layers
    nothing = jnp.zeros((tiles, group, lanes), jnp.float32)

    def step(back, values):
        k = layers - 1 - back
        rows = at_layer(k, group, pitch_of(group))
        lower = lower_ref[:, at_layer(k, group, group), :]
        found = []
        for mode in range(modes):
            value = half_ref[mode, :, rows, :] + lower * values[mode]
            use(mode, k, rows, value)
            found.append(value)
        return tuple(found)

    lax.fori_loop(0, layers, step, (nothing,) * modes)


def put_rows(ref, mode, start, group, result):
    layers = result.shape[0]
    for tile in range(ref.shape[1]):
        ref[mode, tile, pl.ds(start, layers, stride=pitch_of(group)), :] = result[
            :, tile * LANES : (tile + 1) * LANES
        ]


def take_rows(ref, mode, start, group, layers):
    return jnp.concatenate(
        [
            ref[mode, tile, pl.ds(start, layers, stride=pitch_of(group)), :].astype(jnp.bfloat16)
            for tile in range(ref.shape[1])
        ],
        axis=1,
    )


def block_ends_kernel(
    thick_ref, gap_ref, wave_ref, ends_ref, table_ref, factor_ref, velocity_ref, rows_ref,
    saved_ref, out_ref, spectrum_ref, lower_ref, half_ref, end_ref, buffer, arrived, done,
):
    count, part, _, layers = rows_ref.shape
    tiles, group, _ = wave_ref.shape
    if group > part:
        spectrum_ref[...] = jnp.zeros_like(spectrum_ref)

    def fetch(b):
        return pltpu.make_async_copy(rows_ref.at[:, b], buffer.at[b], arrived.at[b])

    for b in range(part):
        fetch(b).start()

    def transform(b, carry):
        fetch(b).wait()
        strips = (factor_ref[b].astype(jnp.float32) * velocity_ref[...]).astype(jnp.bfloat16)
        left = jnp.concatenate([buffer[b, c] for c in range(count)] + [strips], axis=0)
        put_rows(spectrum_ref, 0, b, group, contract(left, table_ref[...], 0, 0))
        return carry

    lax.fori_loop(0, part, transform, 0)
    saving = pltpu.make_async_copy(spectrum_ref, saved_ref, done)
    saving.start()
    eliminate(
        thick_ref, gap_ref, wave_ref, 1,
        lambda mode, k, rows: spectrum_ref[mode, :, rows, :], lower_ref, half_ref,
    )

    def use(mode, k, rows, value):
        for end in range(2):
            end_ref[end, :, pl.ds(k, 1), :] = jnp.sum(
                value * ends_ref[end], axis=1, keepdims=True
            )

    substitute(layers, 1, lower_ref, half_ref, use)
    for end in range(2):
        for tile in range(tiles):
            out_ref[tile * LANES : (tile + 1) * LANES, end * layers : (end + 1) * layers] = (
                end_ref[end, tile].T.astype(jnp.bfloat16)
            )
    saving.wait()


def interface_kernel(
    thick_ref, gap_ref, wave_ref, spread_ref, in_ref,
    out_ref, sum_ref, next_ref, spectrum_ref, lower_ref,
):
    group = wave_ref.shape[1]
    layers = thick_ref.shape[0]
    blocks = spread_ref.shape[0] // 2
    modes = in_ref.shape[0]
    here = in_ref.shape[2] // blocks
    if group > here:
        spectrum_ref[...] = jnp.zeros_like(spectrum_ref)
    for mode in range(modes):
        total = jnp.sum(in_ref[mode].astype(jnp.float32), axis=0)
        for end in range(2):
            sum_ref[end * modes + mode] = total[:, end * layers : (end + 1) * layers]

    for a in range(here):
        picked = pl.ds(a, blocks, stride=here)
        for mode in range(modes):
            left = jnp.concatenate(
                [sum_ref[end * modes + mode, picked, :] for end in range(2)], axis=0
            ).astype(jnp.bfloat16)
            put_rows(spectrum_ref, mode, a, group, contract(left, spread_ref[...], 0, 0))
    eliminate(
        thick_ref, gap_ref, wave_ref, modes,
        lambda mode, k, rows: spectrum_ref[mode, :, rows, :], lower_ref, spectrum_ref,
    )

    def use(mode, k, rows, value):
        spectrum_ref[mode, :, rows, :] = value

    substitute(layers, modes, lower_ref, spectrum_ref, use)
    for a in range(here):
        picked = pl.ds(a, blocks, stride=here)
        for mode in range(modes):
            solved = take_rows(spectrum_ref, mode, a, group, layers)
            found = contract(spread_ref[...], solved, 1, 1)
            for end in range(2):
                next_ref[end * modes + mode, picked, :] = found[
                    end * blocks : (end + 1) * blocks
                ]
    inner = (blocks - 1) * here
    for mode in range(modes):
        first, last = mode, modes + mode
        next_ref[first, here:] = next_ref[first, here:] + sum_ref[last, :inner]
        next_ref[last, :inner] = next_ref[last, :inner] + sum_ref[first, here:]
    for mode in range(modes):
        for end in range(2):
            outgoing = next_ref[end * modes + mode].astype(jnp.bfloat16)
            for copy in range(out_ref.shape[1]):
                out_ref[mode, copy, :, end * layers : (end + 1) * layers] = outgoing


def block_solve_kernel(
    thick_ref, gap_ref, wave_ref, ends_ref, table_ref, factor_ref, velocity_ref, bound_ref,
    saved_ref, out_ref, mass_ref, lower_ref, spectrum_ref, edge_ref, outgoing, arrived, sent,
):
    count, part, x_local, layers = out_ref.shape
    tiles, group, _ = wave_ref.shape
    pieces = arrived.shape[0]
    size = saved_ref.shape[2] // pieces
    loads = []
    for at in range(pieces):
        rows = pl.ds(at * size, size)
        loads.append(
            pltpu.make_async_copy(
                saved_ref.at[:, :, rows], spectrum_ref.at[:, :, rows], arrived.at[at]
            )
        )
        loads[-1].start()
    for end in range(2):
        for tile in range(tiles):
            edge_ref[end, tile] = (
                bound_ref[tile * LANES : (tile + 1) * LANES, end * layers : (end + 1) * layers]
                .astype(jnp.float32)
                .T
            )

    def right_side(mode, k, rows):
        total = spectrum_ref[mode, :, rows, :]
        for end in range(2):
            total = total + ends_ref[end] * edge_ref[end, :, pl.ds(k, 1), :]
        return total

    eliminate(
        thick_ref, gap_ref, wave_ref, 1, right_side, lower_ref, spectrum_ref,
        [load.wait for load in loads],
    )

    def use(mode, k, rows, value):
        spectrum_ref[mode, :, rows, :] = value

    substitute(layers, 1, lower_ref, spectrum_ref, use)

    def send(b):
        return pltpu.make_async_copy(outgoing.at[b], out_ref.at[:, b], sent.at[b])

    def transform(b, at_strips):
        solved = take_rows(spectrum_ref, 0, b, group, layers)
        result = contract(table_ref[...], solved, 1, 1)
        for c in range(count):
            outgoing[b, c] = result[c * x_local : (c + 1) * x_local].astype(jnp.bfloat16)
        send(b).start()
        return at_strips + result[count * x_local :] * factor_ref[b].astype(jnp.float32)

    nothing = jnp.zeros(velocity_ref.shape[1:], jnp.float32)
    at_strips = lax.fori_loop(0, part, transform, nothing)
    for mode in range(velocity_ref.shape[0]):
        mass_ref[mode : mode + 1, :] = jnp.sum(
            at_strips * velocity_ref[mode], axis=0, keepdims=True
        )
    for b in range(part):
        send(b).wait()


def shards(carried, velocity, strip_column, thick):
    modes, x_local, y_local, layers = carried.shape
    count_px = lax.axis_size("px")
    count_py = lax.axis_size("py")
    index_px = lax.axis_index("px")
    index_py = lax.axis_index("py")
    devices = count_px * count_py
    width_x = x_local * count_px
    width_y = y_local * count_py
    pieces = count_px // modes
    part = y_local // pieces
    own_mode, own_piece = index_px // pieces, index_px % pieces
    group = -(-part // 8) * 8
    here = width_x // devices
    group_a = -(-here // 8) * 8
    strip_count = velocity.shape[1] * devices
    both = ("px", "py")

    code = jnp.stack([strip_column // 65536, strip_column // 256 % 256, strip_column % 256])
    code = jnp.pad(code.T, ((0, 0), (0, layers - 3))).astype(jnp.bfloat16)
    packed = jnp.concatenate([velocity, code[None]], axis=0).transpose(1, 0, 2)
    packed = jnp.broadcast_to(packed[None], (devices,) + packed.shape)
    gathered = lax.all_to_all(packed, both, split_axis=0, concat_axis=0, tiled=True)
    gathered = gathered.reshape(strip_count, modes + 1, layers)
    spectra = forward_y(carried, count_px)
    code = gathered[:, modes, :3].astype(jnp.int32)
    column = code[:, 0] * 65536 + code[:, 1] * 256 + code[:, 2]
    all_velocity = gathered[:, :modes].astype(jnp.float32).transpose(1, 0, 2)
    own_velocity = lax.dynamic_index_in_dim(all_velocity, own_mode, 0, False)

    table_x = bf16(sine_table(width_x))
    table_y = jnp.asarray(sine_table(y_local).astype(np.float32))
    local_y = column % width_y - index_py * y_local
    inside = (local_y >= 0) & (local_y < y_local)
    factor = jnp.where(inside[:, None], table_y[jnp.clip(local_y, 0, y_local - 1)], 0.0)
    factor = lax.dynamic_slice_in_dim(factor, own_piece * part, part, axis=1)
    factor = jnp.broadcast_to(factor.T[:, :, None], (part, strip_count, layers))
    factor = factor.astype(jnp.bfloat16)
    table_strips = jnp.concatenate([table_x, table_x[column // width_y]], axis=0)

    gap = jnp.concatenate([2.0 / (thick[:-1] + thick[1:]), 2.0 / thick[-1:]])
    wave_x = jnp.asarray(wave_numbers(width_x).astype(np.float32))
    wave_y = jnp.asarray(wave_numbers(width_y).astype(np.float32))
    wave_block = jnp.asarray(wave_numbers(y_local).astype(np.float32))
    wave_b = lax.dynamic_slice_in_dim(wave_block, own_piece * part, part)
    wave_b = jnp.pad(wave_b, (0, group - part))[:, None] + wave_x.reshape(-1, 1, LANES)
    wave_a = lax.dynamic_slice_in_dim(wave_x, (index_px * count_py + index_py) * here, here)
    wave_a = jnp.pad(wave_a, (0, group_a - here))[:, None] + wave_y.reshape(-1, 1, LANES)
    ends = lax.dynamic_slice_in_dim(table_y[:, (0, y_local - 1)], own_piece * part, part)
    ends = jnp.pad(ends.T, ((0, 0), (0, group - part)))[:, :, None]
    ends = jnp.broadcast_to(ends, (2, group, LANES))

    block_index = np.arange(count_py)
    full = sine_table(width_y)
    not_first = (block_index > 0)[:, None]
    not_last = (block_index < count_py - 1)[:, None]
    before = np.maximum(block_index * y_local - 1, 0)
    after = np.minimum((block_index + 1) * y_local, width_y - 1)
    spread = np.concatenate([full[before] * not_first, full[after] * not_last])

    params = pltpu.CompilerParams(vmem_limit_bytes=VMEM_LIMIT)
    vmem = pl.BlockSpec(memory_space=VMEM)
    smem = pl.BlockSpec(memory_space=SMEM)
    anywhere = pl.BlockSpec(memory_space=pl.ANY)
    float32 = jnp.float32
    tiles_x, tiles_y = width_x // LANES, width_y // LANES

    rows = lax.all_to_all(spectra, "px", split_axis=0, concat_axis=0, tiled=True)
    spectrum, block_ends = pl.pallas_call(
        block_ends_kernel,
        in_specs=[smem, smem] + [vmem] * 5 + [anywhere],
        out_specs=[anywhere, vmem],
        out_shape=[
            jax.ShapeDtypeStruct((1, tiles_x, layers * pitch_of(group), LANES), float32),
            jax.ShapeDtypeStruct((width_x, 2 * layers), jnp.bfloat16),
        ],
        scratch_shapes=[
            pltpu.VMEM((1, tiles_x, layers * pitch_of(group), LANES), float32),
            pltpu.VMEM((tiles_x, layers * group, LANES), float32),
            pltpu.VMEM((1, tiles_x, layers * pitch_of(group), LANES), float32),
            pltpu.VMEM((2, tiles_x, layers, LANES), float32),
            pltpu.VMEM((part, count_px, x_local, layers), jnp.bfloat16),
            pltpu.SemaphoreType.DMA((part,)),
            pltpu.SemaphoreType.DMA(()),
        ],
        compiler_params=params,
        name="block_ends",
    )(thick, gap, wave_b, ends, table_strips, factor, own_velocity, rows)

    arrived = lax.all_to_all(block_ends, both, split_axis=0, concat_axis=0, tiled=True)
    outgoing = pl.pallas_call(
        interface_kernel,
        in_specs=[smem, smem] + [vmem] * 3,
        out_specs=vmem,
        out_shape=jax.ShapeDtypeStruct(
            (modes, pieces, count_py * here, 2 * layers), jnp.bfloat16
        ),
        scratch_shapes=[
            pltpu.VMEM((2 * modes, count_py * here, layers), float32),
            pltpu.VMEM((2 * modes, count_py * here, layers), float32),
            pltpu.VMEM((modes, tiles_y, layers * pitch_of(group_a), LANES), float32),
            pltpu.VMEM((tiles_y, layers * group_a, LANES), float32),
        ],
        compiler_params=pltpu.CompilerParams(vmem_limit_bytes=24 * 1024 * 1024),
        name="interface",
    )(
        thick, gap, wave_a, bf16(spread),
        arrived.reshape(modes, pieces, count_py * here, 2 * layers),
    )
    bounds = lax.all_to_all(
        outgoing.reshape(width_x, 2 * layers), both, split_axis=0, concat_axis=0, tiled=True
    )

    returned, mass = pl.pallas_call(
        block_solve_kernel,
        in_specs=[smem, smem] + [vmem] * 6 + [anywhere],
        out_specs=[anywhere, vmem],
        out_shape=[
            jax.ShapeDtypeStruct((count_px, part, x_local, layers), jnp.bfloat16),
            jax.ShapeDtypeStruct((modes, layers), float32),
        ],
        scratch_shapes=[
            pltpu.VMEM((tiles_x, layers * group, LANES), float32),
            pltpu.VMEM((1, tiles_x, layers * pitch_of(group), LANES), float32),
            pltpu.VMEM((2, tiles_x, layers, LANES), float32),
            pltpu.VMEM((part, count_px, x_local, layers), jnp.bfloat16),
            pltpu.SemaphoreType.DMA((8,)),
            pltpu.SemaphoreType.DMA((part,)),
        ],
        compiler_params=params,
        name="block_solve",
    )(thick, gap, wave_b, ends, table_strips, factor, all_velocity, bounds, spectrum)
    back = lax.all_to_all(returned, "px", split_axis=0, concat_axis=0, tiled=True)
    pressure = inverse_y(back, y_local)
    own_row = (jnp.arange(modes) == own_mode)[:, None]
    local_mass = jnp.where(own_row, jnp.sum(mass * thick[None, :], axis=1)[None, :], 0.0)
    added_mass = lax.psum(lax.psum(local_mass, "py"), "px") / (strip_count * layers)
    return (pressure, added_mass)


def solution(mesh):
    return jax.shard_map(
        shards,
        mesh=mesh,
        in_specs=(P(None, "px", "py", None), P(None, ("px", "py"), None), P(("px", "py")), P()),
        out_specs=(P(None, "px", "py", None), P()),
        check_vma=False,
    )
```

```python
import functools
import math

import jax
import jax.numpy as jnp
import ml_dtypes
import numpy as np
from jax import lax
from jax.experimental import pallas as pl
from jax.experimental.pallas import tpu as pltpu
from jax.sharding import PartitionSpec as P

VMEM_LIMIT = 58 * 1024 * 1024
VMEM = pltpu.MemorySpace.VMEM
SMEM = pltpu.MemorySpace.SMEM
LANES = 128
CHUNK = 64


def sine_table(length):
    steps = np.arange(1, length + 1)
    product = steps[:, None] * steps[None, :] % (2 * (length + 1))
    return math.sqrt(2.0 / (length + 1)) * np.sin(product * (math.pi / (length + 1)))


def wave_numbers(length):
    return 4.0 * np.sin(np.arange(1, length + 1) * (math.pi / (2 * (length + 1)))) ** 2


def bf16(table):
    return jnp.asarray(table.astype(ml_dtypes.bfloat16))


def contract(left, right, left_dim, right_dim):
    return lax.dot_general(
        left, right, (((left_dim,), (right_dim,)), ((), ())), preferred_element_type=jnp.float32
    )


def pitch_of(group):
    return group if group // 8 % 2 else group + 8


def forward_y_kernel(table_ref, grid_ref, out_ref, scratch):
    _, x_chunk, rows, layers = grid_ref.shape
    pieces, part = out_ref.shape[:2]
    group = table_ref.shape[0] // rows
    for start in range(0, x_chunk, group):
        block = grid_ref[0, start : start + group].reshape(group * rows, layers)
        result = contract(table_ref[...], block, 1, 0)
        for at in range(group):
            scratch[pl.ds(start + at, rows, stride=pitch_of(x_chunk)), :] = result[
                at * rows : (at + 1) * rows
            ]
    for b in range(rows):
        begin = b * pitch_of(x_chunk)
        out_ref[b // part, b % part] = scratch[begin : begin + x_chunk, :].astype(jnp.bfloat16)


def inverse_y_kernel(table_ref, in_ref, out_ref, scratch):
    _, x_chunk, rows, layers = out_ref.shape
    group = table_ref.shape[0] // rows
    part = in_ref.shape[1]
    for b in range(rows):
        begin = b * pitch_of(x_chunk)
        scratch[begin : begin + x_chunk, :] = in_ref[b // part, b % part].astype(jnp.float32)
    for start in range(0, x_chunk, group):
        block = jnp.concatenate(
            [
                scratch[pl.ds(start + at, rows, stride=pitch_of(x_chunk)), :]
                for at in range(group)
            ],
            axis=0,
        ).astype(jnp.bfloat16)
        result = contract(table_ref[...], block, 1, 0)
        out_ref[0, start : start + group] = result.reshape(group, rows, layers).astype(
            jnp.bfloat16
        )


def y_table(rows):
    group = max(1, 256 // rows)
    return bf16(np.kron(np.eye(group), sine_table(rows)))


def forward_y(carried, count):
    modes, x_local, rows, layers = carried.shape
    chunk = min(CHUNK, x_local)
    pieces = count // modes
    part = rows // pieces
    table = y_table(rows)
    return pl.pallas_call(
        forward_y_kernel,
        grid=(modes, x_local // chunk),
        in_specs=[
            pl.BlockSpec(table.shape, lambda m, i: (0, 0)),
            pl.BlockSpec((1, chunk, rows, layers), lambda m, i: (m, i, 0, 0)),
        ],
        out_specs=pl.BlockSpec((pieces, part, chunk, layers), lambda m, i: (m, 0, i, 0)),
        out_shape=jax.ShapeDtypeStruct((count, part, x_local, layers), jnp.bfloat16),
        scratch_shapes=[pltpu.VMEM(((rows + 1) * pitch_of(chunk), layers), jnp.float32)],
        compiler_params=pltpu.CompilerParams(vmem_limit_bytes=VMEM_LIMIT),
        name="forward_y",
    )(table, carried)


def inverse_y(spectra, rows):
    count, part, x_local, layers = spectra.shape
    pieces = rows // part
    modes = count // pieces
    chunk = min(CHUNK, x_local)
    table = y_table(rows)
    return pl.pallas_call(
        inverse_y_kernel,
        grid=(modes, x_local // chunk),
        in_specs=[
            pl.BlockSpec(table.shape, lambda m, i: (0, 0)),
            pl.BlockSpec((pieces, part, chunk, layers), lambda m, i: (m, 0, i, 0)),
        ],
        out_specs=pl.BlockSpec((1, chunk, rows, layers), lambda m, i: (m, i, 0, 0)),
        out_shape=jax.ShapeDtypeStruct((modes, x_local, rows, layers), jnp.bfloat16),
        scratch_shapes=[pltpu.VMEM(((rows + 1) * pitch_of(chunk), layers), jnp.float32)],
        compiler_params=pltpu.CompilerParams(vmem_limit_bytes=VMEM_LIMIT),
        name="inverse_y",
    )(table, spectra)


def at_layer(k, group, pitch):
    return pl.ds(pl.multiple_of(k * pitch, 8), group)


def eliminate(
    thick_ref, gap_ref, wave_ref, modes, right_side, lower_ref, half_ref, ready=(None,)
):
    layers = thick_ref.shape[0]
    group = wave_ref.shape[1]
    nothing = jnp.zeros(wave_ref.shape, jnp.float32)

    def step(k, carry):
        excess, sums = carry
        thick, inv_gap = thick_ref[k], gap_ref[k]
        spare = wave_ref[...] * thick + excess
        inverse = 1.0 / (spare + inv_gap)
        lower = inverse * inv_gap
        rows = at_layer(k, group, pitch_of(group))
        lower_ref[:, at_layer(k, group, group), :] = lower
        following = []
        for mode in range(modes):
            total = right_side(mode, k, rows) * thick + sums[mode]
            half_ref[mode, :, rows, :] = total * inverse
            following.append(total * lower)
        return (lower * spare, tuple(following))

    carry = (nothing, (nothing,) * modes)
    each = layers // len(ready)
    for at, wait in enumerate(ready):
        if wait is not None:
            wait()
        carry = lax.fori_loop(at * each, (at + 1) * each, step, carry, unroll=4)


def substitute(layers, modes, lower_ref, half_ref, use):
    tiles, all_rows, lanes = lower_ref.shape
    group = all_rows // layers
    nothing = jnp.zeros((tiles, group, lanes), jnp.float32)

    def step(back, values):
        k = layers - 1 - back
        rows = at_layer(k, group, pitch_of(group))
        lower = lower_ref[:, at_layer(k, group, group), :]
        found = []
        for mode in range(modes):
            value = half_ref[mode, :, rows, :] + lower * values[mode]
            use(mode, k, rows, value)
            found.append(value)
        return tuple(found)

    lax.fori_loop(0, layers, step, (nothing,) * modes, unroll=4)


def put_rows(ref, mode, start, group, result):
    layers = result.shape[0]
    for tile in range(ref.shape[1]):
        ref[mode, tile, pl.ds(start, layers, stride=pitch_of(group)), :] = result[
            :, tile * LANES : (tile + 1) * LANES
        ]


def take_rows(ref, mode, start, group, layers):
    return jnp.concatenate(
        [
            ref[mode, tile, pl.ds(start, layers, stride=pitch_of(group)), :].astype(jnp.bfloat16)
            for tile in range(ref.shape[1])
        ],
        axis=1,
    )


def block_ends_kernel(
    thick_ref, gap_ref, wave_ref, ends_ref, table_ref, strip_table_ref, factor_ref, velocity_ref,
    rows_ref,
    saved_ref, out_ref, spectrum_ref, lower_ref, half_ref, end_ref, buffer, arrived, done,
):
    count, part, _, layers = rows_ref.shape
    tiles, group, _ = wave_ref.shape
    if group > part:
        spectrum_ref[...] = jnp.zeros_like(spectrum_ref)

    def fetch(b):
        return pltpu.make_async_copy(rows_ref.at[:, b], buffer.at[b], arrived.at[b])

    for b in range(part):
        fetch(b).start()

    def transform(b, carry):
        fetch(b).wait()
        strips = (factor_ref[b] * velocity_ref[...]).astype(jnp.bfloat16)
        left = jnp.concatenate([buffer[b, c] for c in range(count)], axis=0)
        result = contract(left, table_ref[...], 0, 0) + contract(
            strips, strip_table_ref[...], 1, 0
        )
        put_rows(spectrum_ref, 0, b, group, result)
        return carry

    lax.fori_loop(0, part, transform, 0, unroll=2)
    saving = pltpu.make_async_copy(spectrum_ref, saved_ref, done)
    saving.start()
    eliminate(
        thick_ref, gap_ref, wave_ref, 1,
        lambda mode, k, rows: spectrum_ref[mode, :, rows, :], lower_ref, half_ref,
    )

    def use(mode, k, rows, value):
        for end in range(2):
            end_ref[end, :, pl.ds(k, 1), :] = jnp.sum(
                value * ends_ref[end], axis=1, keepdims=True
            )

    substitute(layers, 1, lower_ref, half_ref, use)
    for end in range(2):
        for tile in range(tiles):
            out_ref[tile * LANES : (tile + 1) * LANES, end * layers : (end + 1) * layers] = (
                end_ref[end, tile].T.astype(jnp.bfloat16)
            )
    saving.wait()


def interface_kernel(
    thick_ref, gap_ref, wave_ref, spread_ref, in_ref,
    out_ref, sum_ref, next_ref, spectrum_ref, lower_ref,
):
    group = wave_ref.shape[1]
    layers = thick_ref.shape[0]
    blocks = spread_ref.shape[0] // 2
    modes = in_ref.shape[0]
    here = in_ref.shape[2] // blocks
    if group > here:
        spectrum_ref[...] = jnp.zeros_like(spectrum_ref)
    for mode in range(modes):
        total = jnp.sum(in_ref[mode].astype(jnp.float32), axis=0)
        for end in range(2):
            sum_ref[end * modes + mode, : total.shape[0]] = total[:, end * layers : (end + 1) * layers]

    for a in range(here):
        picked = pl.ds(a, blocks, stride=here)
        for mode in range(modes):
            left = jnp.concatenate(
                [sum_ref[end * modes + mode, picked, :] for end in range(2)], axis=0
            ).astype(jnp.bfloat16)
            put_rows(spectrum_ref, mode, a, group, contract(left, spread_ref[...], 0, 0))
    eliminate(
        thick_ref, gap_ref, wave_ref, modes,
        lambda mode, k, rows: spectrum_ref[mode, :, rows, :], lower_ref, spectrum_ref,
    )

    def use(mode, k, rows, value):
        spectrum_ref[mode, :, rows, :] = value

    substitute(layers, modes, lower_ref, spectrum_ref, use)
    for a in range(here):
        picked = pl.ds(a, blocks, stride=here)
        for mode in range(modes):
            solved = take_rows(spectrum_ref, mode, a, group, layers)
            found = contract(spread_ref[...], solved, 1, 1)
            for end in range(2):
                next_ref[end * modes + mode, picked, :] = found[
                    end * blocks : (end + 1) * blocks
                ]
    inner, every = (blocks - 1) * here, blocks * here
    for mode in range(modes):
        first, last = mode, modes + mode
        next_ref[first, here:every] = next_ref[first, here:every] + sum_ref[last, :inner]
        next_ref[last, :inner] = next_ref[last, :inner] + sum_ref[first, here:every]
    for mode in range(modes):
        for end in range(2):
            outgoing = next_ref[end * modes + mode, :every].astype(jnp.bfloat16)
            for copy in range(out_ref.shape[1]):
                out_ref[mode, copy, :, end * layers : (end + 1) * layers] = outgoing


def block_solve_kernel(
    thick_ref, gap_ref, wave_ref, ends_ref, table_ref, strip_table_ref, factor_ref, velocity_ref,
    bound_ref,
    saved_ref, out_ref, mass_ref, lower_ref, spectrum_ref, edge_ref, outgoing, arrived, sent,
):
    count, part, x_local, layers = out_ref.shape
    tiles, group, _ = wave_ref.shape
    pieces = arrived.shape[0]
    size = layers * pitch_of(group) // pieces
    loads = []
    for at in range(pieces):
        rows = pl.ds(at * size, size)
        loads.append(
            pltpu.make_async_copy(
                saved_ref.at[:, :, rows], spectrum_ref.at[:, :, rows], arrived.at[at]
            )
        )
        loads[-1].start()
    for end in range(2):
        for tile in range(tiles):
            edge_ref[end, tile] = (
                bound_ref[tile * LANES : (tile + 1) * LANES, end * layers : (end + 1) * layers]
                .astype(jnp.float32)
                .T
            )

    def right_side(mode, k, rows):
        total = spectrum_ref[mode, :, rows, :]
        for end in range(2):
            total = total + ends_ref[end] * edge_ref[end, :, pl.ds(k, 1), :]
        return total

    eliminate(
        thick_ref, gap_ref, wave_ref, 1, right_side, lower_ref, spectrum_ref,
        [load.wait for load in loads],
    )

    def use(mode, k, rows, value):
        spectrum_ref[mode, :, rows, :] = value

    substitute(layers, 1, lower_ref, spectrum_ref, use)

    def send(b):
        return pltpu.make_async_copy(outgoing.at[b], out_ref.at[:, b], sent.at[b])

    def transform(pair, at_strips):
        first = pair * 2
        solved = jnp.concatenate(
            [take_rows(spectrum_ref, 0, first + at, group, layers) for at in range(2)], axis=0
        )
        result = contract(table_ref[...], solved, 1, 1)
        for at in range(2):
            b = first + at
            found = result[:, at * layers : (at + 1) * layers]
            for c in range(count):
                outgoing[b, c] = found[c * x_local : (c + 1) * x_local].astype(jnp.bfloat16)
            send(b).start()
        found = contract(solved, strip_table_ref[...], 1, 1)
        for at in range(2):
            at_strips += found[at * layers : (at + 1) * layers] * factor_ref[first + at]
        return at_strips

    nothing = jnp.zeros(velocity_ref.shape[1:], jnp.float32)
    at_strips = lax.fori_loop(0, part // 2, transform, nothing, unroll=4)
    for mode in range(velocity_ref.shape[0]):
        mass_ref[mode] = at_strips * velocity_ref[mode]
    for b in range(part):
        send(b).wait()


def shards(carried, velocity, strip_column, thick):
    modes, x_local, y_local, layers = carried.shape
    count_px = lax.axis_size("px")
    count_py = lax.axis_size("py")
    index_px = lax.axis_index("px")
    index_py = lax.axis_index("py")
    devices = count_px * count_py
    width_x = x_local * count_px
    width_y = y_local * count_py
    pieces = count_px // modes
    part = y_local // pieces
    own_mode, own_piece = index_px // pieces, index_px % pieces
    group = -(-part // 8) * 8
    here = width_x // devices
    group_a = -(-here // 8) * 8
    strip_count = velocity.shape[1] * devices
    both = ("px", "py")

    code = jnp.stack([strip_column // 65536, strip_column // 256 % 256, strip_column % 256])
    code = jnp.pad(code.T, ((0, 0), (0, layers - 3))).astype(jnp.bfloat16)
    packed = jnp.concatenate([velocity, code[None]], axis=0).transpose(1, 0, 2)
    packed = jnp.broadcast_to(packed[None], (devices,) + packed.shape)
    gathered = lax.all_to_all(packed, both, split_axis=0, concat_axis=0, tiled=True)
    gathered = gathered.reshape(strip_count, modes + 1, layers)
    spectra = forward_y(carried, count_px)
    code = gathered[:, modes, :3].astype(jnp.int32)
    column = code[:, 0] * 65536 + code[:, 1] * 256 + code[:, 2]
    all_velocity = gathered[:, :modes].astype(jnp.float32).transpose(1, 2, 0)
    own_velocity = lax.dynamic_index_in_dim(all_velocity, own_mode, 0, False)

    table_x = bf16(sine_table(width_x))
    table_y = jnp.asarray(sine_table(y_local).astype(np.float32))
    local_y = column % width_y - index_py * y_local
    inside = (local_y >= 0) & (local_y < y_local)
    factor = jnp.where(inside[:, None], table_y[jnp.clip(local_y, 0, y_local - 1)], 0.0)
    factor = lax.dynamic_slice_in_dim(factor, own_piece * part, part, axis=1)
    factor = factor.T[:, None, :]
    table_strips = table_x[column // width_y]

    gap = jnp.concatenate([2.0 / (thick[:-1] + thick[1:]), 2.0 / thick[-1:]])
    wave_x = jnp.asarray(wave_numbers(width_x).astype(np.float32))
    wave_y = jnp.asarray(wave_numbers(width_y).astype(np.float32))
    wave_block = jnp.asarray(wave_numbers(y_local).astype(np.float32))
    wave_b = lax.dynamic_slice_in_dim(wave_block, own_piece * part, part)
    wave_b = jnp.pad(wave_b, (0, group - part))[:, None] + wave_x.reshape(-1, 1, LANES)
    wave_a = lax.dynamic_slice_in_dim(wave_x, (index_px * count_py + index_py) * here, here)
    wave_a = jnp.pad(wave_a, (0, group_a - here))[:, None] + wave_y.reshape(-1, 1, LANES)
    ends = lax.dynamic_slice_in_dim(table_y[:, (0, y_local - 1)], own_piece * part, part)
    ends = jnp.pad(ends.T, ((0, 0), (0, group - part)))[:, :, None]
    ends = jnp.broadcast_to(ends, (2, group, LANES))

    block_index = np.arange(count_py)
    full = sine_table(width_y)
    not_first = (block_index > 0)[:, None]
    not_last = (block_index < count_py - 1)[:, None]
    before = np.maximum(block_index * y_local - 1, 0)
    after = np.minimum((block_index + 1) * y_local, width_y - 1)
    spread = np.concatenate([full[before] * not_first, full[after] * not_last])

    params = pltpu.CompilerParams(vmem_limit_bytes=VMEM_LIMIT)
    vmem = pl.BlockSpec(memory_space=VMEM)
    smem = pl.BlockSpec(memory_space=SMEM)
    anywhere = pl.BlockSpec(memory_space=pl.ANY)
    float32 = jnp.float32
    tiles_x, tiles_y = width_x // LANES, width_y // LANES

    rows = lax.all_to_all(spectra, "px", split_axis=0, concat_axis=0, tiled=True)
    spectrum, block_ends = pl.pallas_call(
        block_ends_kernel,
        in_specs=[smem, smem] + [vmem] * 6 + [anywhere],
        out_specs=[anywhere, vmem],
        out_shape=[
            jax.ShapeDtypeStruct((1, tiles_x, (layers + 1) * pitch_of(group), LANES), float32),
            jax.ShapeDtypeStruct((width_x, 2 * layers), jnp.bfloat16),
        ],
        scratch_shapes=[
            pltpu.VMEM((1, tiles_x, (layers + 1) * pitch_of(group), LANES), float32),
            pltpu.VMEM((tiles_x, layers * group, LANES), float32),
            pltpu.VMEM((1, tiles_x, (layers + 1) * pitch_of(group), LANES), float32),
            pltpu.VMEM((2, tiles_x, layers, LANES), float32),
            pltpu.VMEM((part, count_px, x_local, layers), jnp.bfloat16),
            pltpu.SemaphoreType.DMA((part,)),
            pltpu.SemaphoreType.DMA(()),
        ],
        compiler_params=params,
        name="block_ends",
    )(thick, gap, wave_b, ends, table_x, table_strips, factor, own_velocity, rows)

    arrived = lax.all_to_all(block_ends, both, split_axis=0, concat_axis=0, tiled=True)
    outgoing = pl.pallas_call(
        interface_kernel,
        in_specs=[smem, smem] + [vmem] * 3,
        out_specs=vmem,
        out_shape=jax.ShapeDtypeStruct(
            (modes, pieces, count_py * here, 2 * layers), jnp.bfloat16
        ),
        scratch_shapes=[
            pltpu.VMEM((2 * modes, (count_py + 1) * here, layers), float32),
            pltpu.VMEM((2 * modes, (count_py + 1) * here, layers), float32),
            pltpu.VMEM((modes, tiles_y, (layers + 1) * pitch_of(group_a), LANES), float32),
            pltpu.VMEM((tiles_y, layers * group_a, LANES), float32),
        ],
        compiler_params=pltpu.CompilerParams(vmem_limit_bytes=24 * 1024 * 1024),
        name="interface",
    )(
        thick, gap, wave_a, bf16(spread),
        arrived.reshape(modes, pieces, count_py * here, 2 * layers),
    )
    bounds = lax.all_to_all(
        outgoing.reshape(width_x, 2 * layers), both, split_axis=0, concat_axis=0, tiled=True
    )

    returned, mass = pl.pallas_call(
        block_solve_kernel,
        in_specs=[smem, smem] + [vmem] * 7 + [anywhere],
        out_specs=[anywhere, vmem],
        out_shape=[
            jax.ShapeDtypeStruct((count_px, part, x_local, layers), jnp.bfloat16),
            jax.ShapeDtypeStruct((modes, layers, strip_count), float32),
        ],
        scratch_shapes=[
            pltpu.VMEM((tiles_x, layers * group, LANES), float32),
            pltpu.VMEM((1, tiles_x, (layers + 1) * pitch_of(group), LANES), float32),
            pltpu.VMEM((2, tiles_x, layers, LANES), float32),
            pltpu.VMEM((part, count_px, x_local, layers), jnp.bfloat16),
            pltpu.SemaphoreType.DMA((8,)),
            pltpu.SemaphoreType.DMA((part,)),
        ],
        compiler_params=params,
        name="block_solve",
    )(
        thick, gap, wave_b, ends, table_x, table_strips, factor, all_velocity, bounds, spectrum
    )
    back = lax.all_to_all(returned, "px", split_axis=0, concat_axis=0, tiled=True)
    pressure = inverse_y(back, y_local)
    own_row = (jnp.arange(modes) == own_mode)[:, None]
    local_mass = jnp.sum(mass * thick[None, :, None], axis=(1, 2))
    local_mass = jnp.where(own_row, local_mass[None, :], 0.0)
    added_mass = lax.psum(lax.psum(local_mass, "py"), "px") / (strip_count * layers)
    return (pressure, added_mass)


def solution(mesh):
    return jax.shard_map(
        shards,
        mesh=mesh,
        in_specs=(P(None, "px", "py", None), P(None, ("px", "py"), None), P(("px", "py")), P()),
        out_specs=(P(None, "px", "py", None), P()),
        check_vma=False,
    )
```

```python
import functools
import math

import jax
import jax.numpy as jnp
import ml_dtypes
import numpy as np
from jax import lax
from jax.experimental import pallas as pl
from jax.experimental.pallas import tpu as pltpu
from jax.sharding import PartitionSpec as P

VMEM_LIMIT = 58 * 1024 * 1024
VMEM = pltpu.MemorySpace.VMEM
SMEM = pltpu.MemorySpace.SMEM
LANES = 128
CHUNK = 64
BATCH = 8


def sine_table(length):
    steps = np.arange(1, length + 1)
    product = steps[:, None] * steps[None, :] % (2 * (length + 1))
    return math.sqrt(2.0 / (length + 1)) * np.sin(product * (math.pi / (length + 1)))


def wave_numbers(length):
    return 4.0 * np.sin(np.arange(1, length + 1) * (math.pi / (2 * (length + 1)))) ** 2


def bf16(table):
    return jnp.asarray(table.astype(ml_dtypes.bfloat16))


def contract(left, right, left_dim, right_dim):
    return lax.dot_general(
        left, right, (((left_dim,), (right_dim,)), ((), ())), preferred_element_type=jnp.float32
    )


def pitch_of(group):
    return group if group // 8 % 2 else group + 8


def forward_y_kernel(me_ref, table_ref, grid_ref, *refs):
    outs, scratch = refs[:-1], refs[-1]
    _, x_chunk, rows, layers = grid_ref.shape
    part = outs[0].shape[0]
    group = table_ref.shape[0] // rows
    pitch = pitch_of(x_chunk)
    for start in range(0, x_chunk, group):
        block = grid_ref[0, start : start + group].reshape(group * rows, layers)
        result = contract(table_ref[...], block, 1, 0)
        for at in range(group):
            scratch[pl.ds(start + at, rows, stride=pitch), :] = result[
                at * rows : (at + 1) * rows
            ]
    for f, out in enumerate(outs):
        first = (me_ref[1] ^ f) * part
        for b in range(part):
            begin = pl.multiple_of((first + b) * pitch, 8)
            out[b] = scratch[pl.ds(begin, x_chunk), :].astype(jnp.bfloat16)


def inverse_y_kernel(pieces, me_ref, table_ref, *refs):
    ins, out_ref, scratch = refs[:pieces], refs[-2], refs[-1]
    _, x_chunk, rows, layers = out_ref.shape
    part = ins[0].shape[0]
    group = table_ref.shape[0] // rows
    pitch = pitch_of(x_chunk)
    for f, value in enumerate(ins):
        first = (me_ref[1] ^ f) * part
        for b in range(part):
            begin = pl.multiple_of((first + b) * pitch, 8)
            scratch[pl.ds(begin, x_chunk), :] = value[b].astype(jnp.float32)
    for start in range(0, x_chunk, group):
        block = jnp.concatenate(
            [scratch[pl.ds(start + at, rows, stride=pitch), :] for at in range(group)], axis=0
        ).astype(jnp.bfloat16)
        result = contract(table_ref[...], block, 1, 0)
        out_ref[0, start : start + group] = result.reshape(group, rows, layers).astype(
            jnp.bfloat16
        )


def y_table(rows):
    group = max(1, 256 // rows)
    return bf16(np.kron(np.eye(group), sine_table(rows)))


def forward_y(me, carried, pieces, step):
    modes, x_local, rows, layers = carried.shape
    chunk = min(CHUNK, x_local)
    part = rows // pieces
    table = y_table(rows)
    return pl.pallas_call(
        forward_y_kernel,
        grid_spec=pltpu.PrefetchScalarGridSpec(
            num_scalar_prefetch=1,
            grid=(x_local // chunk,),
            in_specs=[
                pl.BlockSpec(table.shape, lambda i, own: (0, 0)),
                pl.BlockSpec((1, chunk, rows, layers), lambda i, own: (own[0] ^ step, i, 0, 0)),
            ],
            out_specs=[pl.BlockSpec((part, chunk, layers), lambda i, own: (0, i, 0))] * pieces,
            scratch_shapes=[pltpu.VMEM(((rows + 1) * pitch_of(chunk), layers), jnp.float32)],
        ),
        out_shape=[jax.ShapeDtypeStruct((part, x_local, layers), jnp.bfloat16)] * pieces,
        compiler_params=pltpu.CompilerParams(vmem_limit_bytes=VMEM_LIMIT),
        name="forward_y",
    )(me, table, carried)


def inverse_y(me, spectra, rows, modes, step, pressure):
    pieces = len(spectra)
    part, x_local, layers = spectra[0].shape
    chunk = min(CHUNK, x_local)
    table = y_table(rows)
    earlier = [] if pressure is None else [pressure]
    return pl.pallas_call(
        functools.partial(inverse_y_kernel, pieces),
        grid_spec=pltpu.PrefetchScalarGridSpec(
            num_scalar_prefetch=1,
            grid=(x_local // chunk,),
            in_specs=[pl.BlockSpec(table.shape, lambda i, own: (0, 0))]
            + [pl.BlockSpec((part, chunk, layers), lambda i, own: (0, i, 0))] * pieces
            + [pl.BlockSpec(memory_space=pl.ANY)] * len(earlier),
            out_specs=pl.BlockSpec(
                (1, chunk, rows, layers), lambda i, own: (own[0] ^ step, i, 0, 0)
            ),
            scratch_shapes=[pltpu.VMEM(((rows + 1) * pitch_of(chunk), layers), jnp.float32)],
        ),
        out_shape=jax.ShapeDtypeStruct((modes, x_local, rows, layers), jnp.bfloat16),
        input_output_aliases={2 + pieces: 0} if earlier else {},
        compiler_params=pltpu.CompilerParams(vmem_limit_bytes=VMEM_LIMIT),
        name="inverse_y",
    )(me, table, *spectra, *earlier)


def swap(values, distance):
    return lax.ppermute(
        values, "px", [(k, k ^ distance) for k in range(lax.axis_size("px"))]
    )


def at_layer(k, group, pitch):
    return pl.ds(pl.multiple_of(k * pitch, 8), group)


def eliminate(
    thick_ref, gap_ref, wave_ref, modes, right_side, lower_ref, half_ref, ready=(None,)
):
    layers = thick_ref.shape[0]
    group = wave_ref.shape[1]
    nothing = jnp.zeros(wave_ref.shape, jnp.float32)

    def step(k, carry):
        excess, sums = carry
        thick, inv_gap = thick_ref[k], gap_ref[k]
        spare = wave_ref[...] * thick + excess
        inverse = 1.0 / (spare + inv_gap)
        lower = inverse * inv_gap
        rows = at_layer(k, group, pitch_of(group))
        lower_ref[:, at_layer(k, group, group), :] = lower
        following = []
        for mode in range(modes):
            total = right_side(mode, k, rows) * thick + sums[mode]
            half_ref[mode, :, rows, :] = total * inverse
            following.append(total * lower)
        return (lower * spare, tuple(following))

    carry = (nothing, (nothing,) * modes)
    each = layers // len(ready)
    for at, wait in enumerate(ready):
        if wait is not None:
            wait()
        carry = lax.fori_loop(at * each, (at + 1) * each, step, carry, unroll=4)


def substitute(layers, modes, lower_ref, half_ref, use):
    tiles, all_rows, lanes = lower_ref.shape
    group = all_rows // layers
    nothing = jnp.zeros((tiles, group, lanes), jnp.float32)

    def step(back, values):
        k = layers - 1 - back
        rows = at_layer(k, group, pitch_of(group))
        lower = lower_ref[:, at_layer(k, group, group), :]
        found = []
        for mode in range(modes):
            value = half_ref[mode, :, rows, :] + lower * values[mode]
            use(mode, k, rows, value)
            found.append(value)
        return tuple(found)

    lax.fori_loop(0, layers, step, (nothing,) * modes, unroll=4)


def put_rows(ref, mode, start, group, result):
    layers = result.shape[0]
    for tile in range(ref.shape[1]):
        ref[mode, tile, pl.ds(start, layers, stride=pitch_of(group)), :] = result[
            :, tile * LANES : (tile + 1) * LANES
        ]


def take_rows(ref, mode, start, group, layers):
    return jnp.concatenate(
        [
            ref[mode, tile, pl.ds(start, layers, stride=pitch_of(group)), :].astype(jnp.bfloat16)
            for tile in range(ref.shape[1])
        ],
        axis=1,
    )


def block_ends_kernel(
    count, me_ref, thick_ref, gap_ref, wave_ref, ends_ref, table_ref, strip_table_ref, factor_ref, velocity_ref,
    *refs,
):
    rows_refs, (saved_ref, out_ref, spectrum_ref, lower_ref, half_ref) = refs[:count], refs[count : count + 5]
    end_ref, buffer, arrived, done = refs[count + 5 :]
    part, _, layers = rows_refs[0].shape
    each = min(BATCH, part)
    me = me_ref[0]
    tiles, group, _ = wave_ref.shape
    if group > part:
        spectrum_ref[...] = jnp.zeros_like(spectrum_ref)

    def fetch(at, d):
        some = pl.ds(at * each, each)
        return pltpu.make_async_copy(
            rows_refs[d].at[some], buffer.at[me ^ d, some], arrived.at[at, d]
        )

    for at in range(part // each):
        for d in range(count):
            fetch(at, d).start()

    def transform(b, carry):
        strips = (factor_ref[b] * velocity_ref[...]).astype(jnp.bfloat16)
        left = jnp.concatenate([buffer[c, b] for c in range(count)], axis=0)
        result = contract(left, table_ref[...], 0, 0) + contract(
            strips, strip_table_ref[...], 1, 0
        )
        put_rows(spectrum_ref, 0, b, group, result)
        return carry

    for at in range(part // each):
        for d in range(count):
            fetch(at, d).wait()
        lax.fori_loop(at * each, (at + 1) * each, transform, 0, unroll=2)
    saving = pltpu.make_async_copy(spectrum_ref, saved_ref, done)
    saving.start()
    eliminate(
        thick_ref, gap_ref, wave_ref, 1,
        lambda mode, k, rows: spectrum_ref[mode, :, rows, :], lower_ref, half_ref,
    )

    def use(mode, k, rows, value):
        for end in range(2):
            end_ref[end, :, pl.ds(k, 1), :] = jnp.sum(
                value * ends_ref[end], axis=1, keepdims=True
            )

    substitute(layers, 1, lower_ref, half_ref, use)
    for end in range(2):
        for tile in range(tiles):
            out_ref[tile * LANES : (tile + 1) * LANES, end * layers : (end + 1) * layers] = (
                end_ref[end, tile].T.astype(jnp.bfloat16)
            )
    saving.wait()


def interface_kernel(
    thick_ref, gap_ref, wave_ref, spread_ref, in_ref,
    out_ref, sum_ref, next_ref, spectrum_ref, lower_ref,
):
    group = wave_ref.shape[1]
    layers = thick_ref.shape[0]
    blocks = spread_ref.shape[0] // 2
    modes = in_ref.shape[0]
    here = in_ref.shape[2] // blocks
    if group > here:
        spectrum_ref[...] = jnp.zeros_like(spectrum_ref)
    for mode in range(modes):
        total = jnp.sum(in_ref[mode].astype(jnp.float32), axis=0)
        for end in range(2):
            sum_ref[end * modes + mode, : total.shape[0]] = total[:, end * layers : (end + 1) * layers]

    for a in range(here):
        picked = pl.ds(a, blocks, stride=here)
        for mode in range(modes):
            left = jnp.concatenate(
                [sum_ref[end * modes + mode, picked, :] for end in range(2)], axis=0
            ).astype(jnp.bfloat16)
            put_rows(spectrum_ref, mode, a, group, contract(left, spread_ref[...], 0, 0))
    eliminate(
        thick_ref, gap_ref, wave_ref, modes,
        lambda mode, k, rows: spectrum_ref[mode, :, rows, :], lower_ref, spectrum_ref,
    )

    def use(mode, k, rows, value):
        spectrum_ref[mode, :, rows, :] = value

    substitute(layers, modes, lower_ref, spectrum_ref, use)
    for a in range(here):
        picked = pl.ds(a, blocks, stride=here)
        for mode in range(modes):
            solved = take_rows(spectrum_ref, mode, a, group, layers)
            found = contract(spread_ref[...], solved, 1, 1)
            for end in range(2):
                next_ref[end * modes + mode, picked, :] = found[
                    end * blocks : (end + 1) * blocks
                ]
    inner, every = (blocks - 1) * here, blocks * here
    for mode in range(modes):
        first, last = mode, modes + mode
        next_ref[first, here:every] = next_ref[first, here:every] + sum_ref[last, :inner]
        next_ref[last, :inner] = next_ref[last, :inner] + sum_ref[first, here:every]
    for mode in range(modes):
        for end in range(2):
            outgoing = next_ref[end * modes + mode, :every].astype(jnp.bfloat16)
            for copy in range(out_ref.shape[1]):
                out_ref[mode, copy, :, end * layers : (end + 1) * layers] = outgoing


def block_solve_kernel(
    count, me_ref, thick_ref, gap_ref, wave_ref, ends_ref, table_ref, strip_table_ref, factor_ref, velocity_ref,
    bound_ref,
    saved_ref, *refs,
):
    outs, (mass_ref, lower_ref, spectrum_ref, edge_ref) = refs[:count], refs[count : count + 4]
    outgoing, arrived, sent = refs[count + 4 :]
    part, x_local, layers = outs[0].shape
    each = min(BATCH, part)
    me = me_ref[0]
    tiles, group, _ = wave_ref.shape
    pieces = arrived.shape[0]
    size = layers * pitch_of(group) // pieces
    loads = []
    for at in range(pieces):
        rows = pl.ds(at * size, size)
        loads.append(
            pltpu.make_async_copy(
                saved_ref.at[:, :, rows], spectrum_ref.at[:, :, rows], arrived.at[at]
            )
        )
        loads[-1].start()
    for end in range(2):
        for tile in range(tiles):
            edge_ref[end, tile] = (
                bound_ref[tile * LANES : (tile + 1) * LANES, end * layers : (end + 1) * layers]
                .astype(jnp.float32)
                .T
            )

    def right_side(mode, k, rows):
        total = spectrum_ref[mode, :, rows, :]
        for end in range(2):
            total = total + ends_ref[end] * edge_ref[end, :, pl.ds(k, 1), :]
        return total

    eliminate(
        thick_ref, gap_ref, wave_ref, 1, right_side, lower_ref, spectrum_ref,
        [load.wait for load in loads],
    )

    def use(mode, k, rows, value):
        spectrum_ref[mode, :, rows, :] = value

    substitute(layers, 1, lower_ref, spectrum_ref, use)

    def send(at, d):
        some = pl.ds(at * each, each)
        return pltpu.make_async_copy(outgoing.at[me ^ d, some], outs[d].at[some], sent.at[at, d])

    def transform(pair, at_strips):
        first = pair * 2
        solved = jnp.concatenate(
            [take_rows(spectrum_ref, 0, first + at, group, layers) for at in range(2)], axis=0
        )
        result = contract(table_ref[...], solved, 1, 1)
        for at in range(2):
            b = first + at
            found = result[:, at * layers : (at + 1) * layers]
            for c in range(count):
                outgoing[c, b] = found[c * x_local : (c + 1) * x_local].astype(jnp.bfloat16)
        found = contract(solved, strip_table_ref[...], 1, 1)
        for at in range(2):
            at_strips += found[at * layers : (at + 1) * layers] * factor_ref[first + at]
        return at_strips

    nothing = jnp.zeros(velocity_ref.shape[1:], jnp.float32)
    at_strips = nothing
    for at in range(part // each):
        at_strips = lax.fori_loop(
            at * each // 2, (at + 1) * each // 2, transform, at_strips, unroll=True
        )
        for d in range(count):
            send(at, d).start()
    for mode in range(velocity_ref.shape[0]):
        mass_ref[mode] = at_strips * velocity_ref[mode]
    for at in range(part // each):
        for d in range(count):
            send(at, d).wait()


def shards(carried, velocity, strip_column, thick):
    modes, x_local, y_local, layers = carried.shape
    count_px = lax.axis_size("px")
    count_py = lax.axis_size("py")
    index_px = lax.axis_index("px")
    index_py = lax.axis_index("py")
    devices = count_px * count_py
    width_x = x_local * count_px
    width_y = y_local * count_py
    pieces = count_px // modes
    part = y_local // pieces
    own_mode, own_piece = index_px // pieces, index_px % pieces
    group = -(-part // 8) * 8
    here = width_x // devices
    group_a = -(-here // 8) * 8
    strip_count = velocity.shape[1] * devices
    both = ("px", "py")

    code = jnp.stack([strip_column // 65536, strip_column // 256 % 256, strip_column % 256])
    code = jnp.pad(code.T, ((0, 0), (0, layers - 3))).astype(jnp.bfloat16)
    packed = jnp.concatenate([velocity, code[None]], axis=0).transpose(1, 0, 2)
    packed = jnp.broadcast_to(packed[None], (devices,) + packed.shape)
    gathered = lax.all_to_all(packed, both, split_axis=0, concat_axis=0, tiled=True)
    gathered = gathered.reshape(strip_count, modes + 1, layers)
    own = index_px.astype(jnp.int32).reshape(1)
    place = jnp.stack([own_mode, own_piece]).astype(jnp.int32)
    rows = [None] * count_px
    for step in reversed(range(modes)):
        chunks = forward_y(place, carried, pieces, step)
        for f, chunk in enumerate(chunks):
            d = step * pieces + f
            rows[d] = swap(chunk, d) if d else chunk
    code = gathered[:, modes, :3].astype(jnp.int32)
    column = code[:, 0] * 65536 + code[:, 1] * 256 + code[:, 2]
    all_velocity = gathered[:, :modes].astype(jnp.float32).transpose(1, 2, 0)
    own_velocity = lax.dynamic_index_in_dim(all_velocity, own_mode, 0, False)

    table_x = bf16(sine_table(width_x))
    table_y = jnp.asarray(sine_table(y_local).astype(np.float32))
    local_y = column % width_y - index_py * y_local
    inside = (local_y >= 0) & (local_y < y_local)
    factor = jnp.where(inside[:, None], table_y[jnp.clip(local_y, 0, y_local - 1)], 0.0)
    factor = lax.dynamic_slice_in_dim(factor, own_piece * part, part, axis=1)
    factor = factor.T[:, None, :]
    table_strips = table_x[column // width_y]

    gap = jnp.concatenate([2.0 / (thick[:-1] + thick[1:]), 2.0 / thick[-1:]])
    wave_x = jnp.asarray(wave_numbers(width_x).astype(np.float32))
    wave_y = jnp.asarray(wave_numbers(width_y).astype(np.float32))
    wave_block = jnp.asarray(wave_numbers(y_local).astype(np.float32))
    wave_b = lax.dynamic_slice_in_dim(wave_block, own_piece * part, part)
    wave_b = jnp.pad(wave_b, (0, group - part))[:, None] + wave_x.reshape(-1, 1, LANES)
    wave_a = lax.dynamic_slice_in_dim(wave_x, (index_px * count_py + index_py) * here, here)
    wave_a = jnp.pad(wave_a, (0, group_a - here))[:, None] + wave_y.reshape(-1, 1, LANES)
    ends = lax.dynamic_slice_in_dim(table_y[:, (0, y_local - 1)], own_piece * part, part)
    ends = jnp.pad(ends.T, ((0, 0), (0, group - part)))[:, :, None]
    ends = jnp.broadcast_to(ends, (2, group, LANES))

    block_index = np.arange(count_py)
    full = sine_table(width_y)
    not_first = (block_index > 0)[:, None]
    not_last = (block_index < count_py - 1)[:, None]
    before = np.maximum(block_index * y_local - 1, 0)
    after = np.minimum((block_index + 1) * y_local, width_y - 1)
    spread = np.concatenate([full[before] * not_first, full[after] * not_last])

    params = pltpu.CompilerParams(vmem_limit_bytes=VMEM_LIMIT)
    vmem = pl.BlockSpec(memory_space=VMEM)
    smem = pl.BlockSpec(memory_space=SMEM)
    anywhere = pl.BlockSpec(memory_space=pl.ANY)
    float32 = jnp.float32
    tiles_x, tiles_y = width_x // LANES, width_y // LANES

    spectrum, block_ends = pl.pallas_call(
        functools.partial(block_ends_kernel, count_px),
        in_specs=[smem] * 3 + [vmem] * 6 + [anywhere] * count_px,
        out_specs=[anywhere, vmem],
        out_shape=[
            jax.ShapeDtypeStruct((1, tiles_x, (layers + 1) * pitch_of(group), LANES), float32),
            jax.ShapeDtypeStruct((width_x, 2 * layers), jnp.bfloat16),
        ],
        scratch_shapes=[
            pltpu.VMEM((1, tiles_x, (layers + 1) * pitch_of(group), LANES), float32),
            pltpu.VMEM((tiles_x, layers * group, LANES), float32),
            pltpu.VMEM((1, tiles_x, (layers + 1) * pitch_of(group), LANES), float32),
            pltpu.VMEM((2, tiles_x, layers, LANES), float32),
            pltpu.VMEM((count_px, part, x_local, layers), jnp.bfloat16),
            pltpu.SemaphoreType.DMA((part // min(BATCH, part), count_px)),
            pltpu.SemaphoreType.DMA(()),
        ],
        compiler_params=params,
        name="block_ends",
    )(own, thick, gap, wave_b, ends, table_x, table_strips, factor, own_velocity, *rows)

    arrived = lax.all_to_all(block_ends, both, split_axis=0, concat_axis=0, tiled=True)
    outgoing = pl.pallas_call(
        interface_kernel,
        in_specs=[smem, smem] + [vmem] * 3,
        out_specs=vmem,
        out_shape=jax.ShapeDtypeStruct(
            (modes, pieces, count_py * here, 2 * layers), jnp.bfloat16
        ),
        scratch_shapes=[
            pltpu.VMEM((2 * modes, (count_py + 1) * here, layers), float32),
            pltpu.VMEM((2 * modes, (count_py + 1) * here, layers), float32),
            pltpu.VMEM((modes, tiles_y, (layers + 1) * pitch_of(group_a), LANES), float32),
            pltpu.VMEM((tiles_y, layers * group_a, LANES), float32),
        ],
        compiler_params=pltpu.CompilerParams(vmem_limit_bytes=24 * 1024 * 1024),
        name="interface",
    )(
        thick, gap, wave_a, bf16(spread),
        arrived.reshape(modes, pieces, count_py * here, 2 * layers),
    )
    bounds = lax.all_to_all(
        outgoing.reshape(width_x, 2 * layers), both, split_axis=0, concat_axis=0, tiled=True
    )

    *returned, mass = pl.pallas_call(
        functools.partial(block_solve_kernel, count_px),
        in_specs=[smem] * 3 + [vmem] * 7 + [anywhere],
        out_specs=[anywhere] * count_px + [vmem],
        out_shape=[jax.ShapeDtypeStruct((part, x_local, layers), jnp.bfloat16)] * count_px
        + [
            jax.ShapeDtypeStruct((modes, layers, strip_count), float32),
        ],
        scratch_shapes=[
            pltpu.VMEM((tiles_x, layers * group, LANES), float32),
            pltpu.VMEM((1, tiles_x, (layers + 1) * pitch_of(group), LANES), float32),
            pltpu.VMEM((2, tiles_x, layers, LANES), float32),
            pltpu.VMEM((count_px, part, x_local, layers), jnp.bfloat16),
            pltpu.SemaphoreType.DMA((8,)),
            pltpu.SemaphoreType.DMA((part // min(BATCH, part), count_px)),
        ],
        compiler_params=params,
        name="block_solve",
    )(
        own, thick, gap, wave_b, ends, table_x, table_strips, factor, all_velocity, bounds,
        spectrum,
    )
    back = [swap(chunk, d) if d else chunk for d, chunk in enumerate(returned)]
    own_row = (jnp.arange(modes) == own_mode)[:, None]
    local_mass = jnp.sum(mass * thick[None, :, None], axis=(1, 2))
    local_mass = jnp.where(own_row, local_mass[None, :], 0.0)
    local_mass = lax.psum(local_mass, "py")
    pressure = None
    for step in range(modes):
        chunks = back[step * pieces : (step + 1) * pieces]
        pressure = inverse_y(place, chunks, y_local, modes, step, pressure)
        if step == 0:
            pressure, local_mass = lax.optimization_barrier((pressure, local_mass))
            every_mass = lax.all_gather(local_mass, "px", axis=0, tiled=False)
    added_mass = jnp.sum(every_mass, axis=0) / (strip_count * layers)
    return (pressure, added_mass)


def solution(mesh):
    return jax.shard_map(
        shards,
        mesh=mesh,
        in_specs=(P(None, "px", "py", None), P(None, ("px", "py"), None), P(("px", "py")), P()),
        out_specs=(P(None, "px", "py", None), P()),
        check_vma=False,
    )
```

```python
import functools
import math

import jax
import jax.numpy as jnp
import ml_dtypes
import numpy as np
from jax import lax
from jax.experimental import pallas as pl
from jax.experimental.pallas import tpu as pltpu
from jax.sharding import PartitionSpec as P

VMEM_LIMIT = 58 * 1024 * 1024
VMEM = pltpu.MemorySpace.VMEM
SMEM = pltpu.MemorySpace.SMEM
LANES = 128
INVERSE_LIMIT = 16 * 1024 * 1024
CHUNK = 64
BATCH = 8


def sine_table(length):
    steps = np.arange(1, length + 1)
    product = steps[:, None] * steps[None, :] % (2 * (length + 1))
    return math.sqrt(2.0 / (length + 1)) * np.sin(product * (math.pi / (length + 1)))


def wave_numbers(length):
    return 4.0 * np.sin(np.arange(1, length + 1) * (math.pi / (2 * (length + 1)))) ** 2


def bf16(table):
    return jnp.asarray(table.astype(ml_dtypes.bfloat16))


def contract(left, right, left_dim, right_dim):
    return lax.dot_general(
        left, right, (((left_dim,), (right_dim,)), ((), ())), preferred_element_type=jnp.float32
    )


def pitch_of(group):
    return group if group // 8 % 2 else group + 8


def forward_y_kernel(me_ref, table_ref, grid_ref, *refs):
    outs, scratch = refs[:-1], refs[-1]
    _, x_chunk, rows, layers = grid_ref.shape
    part = outs[0].shape[0]
    group = table_ref.shape[0] // rows
    pitch = pitch_of(x_chunk)
    for start in range(0, x_chunk, group):
        block = grid_ref[0, start : start + group].reshape(group * rows, layers)
        result = contract(table_ref[...], block, 1, 0)
        for at in range(group):
            scratch[pl.ds(start + at, rows, stride=pitch), :] = result[
                at * rows : (at + 1) * rows
            ]
    for f, out in enumerate(outs):
        first = (me_ref[1] ^ f) * part
        for b in range(part):
            begin = pl.multiple_of((first + b) * pitch, 8)
            out[b] = scratch[pl.ds(begin, x_chunk), :].astype(jnp.bfloat16)


def inverse_y_kernel(pieces, me_ref, table_ref, *refs):
    ins, out_ref, scratch = refs[:pieces], refs[-2], refs[-1]
    _, x_chunk, rows, layers = out_ref.shape
    part = ins[0].shape[0]
    group = table_ref.shape[0] // rows
    pitch = pitch_of(x_chunk)
    for f, value in enumerate(ins):
        first = (me_ref[1] ^ f) * part
        for b in range(part):
            begin = pl.multiple_of((first + b) * pitch, 8)
            scratch[pl.ds(begin, x_chunk), :] = value[b].astype(jnp.float32)
    for start in range(0, x_chunk, group):
        block = jnp.concatenate(
            [scratch[pl.ds(start + at, rows, stride=pitch), :] for at in range(group)], axis=0
        ).astype(jnp.bfloat16)
        result = contract(table_ref[...], block, 1, 0)
        out_ref[0, start : start + group] = result.reshape(group, rows, layers).astype(
            jnp.bfloat16
        )


def y_table(rows):
    group = max(1, 256 // rows)
    return bf16(np.kron(np.eye(group), sine_table(rows)))


def forward_y(me, carried, pieces, step):
    modes, x_local, rows, layers = carried.shape
    chunk = min(CHUNK, x_local)
    part = rows // pieces
    table = y_table(rows)
    return pl.pallas_call(
        forward_y_kernel,
        grid_spec=pltpu.PrefetchScalarGridSpec(
            num_scalar_prefetch=1,
            grid=(x_local // chunk,),
            in_specs=[
                pl.BlockSpec(table.shape, lambda i, own: (0, 0)),
                pl.BlockSpec((1, chunk, rows, layers), lambda i, own: (own[0] ^ step, i, 0, 0)),
            ],
            out_specs=[pl.BlockSpec((part, chunk, layers), lambda i, own: (0, i, 0))] * pieces,
            scratch_shapes=[pltpu.VMEM(((rows + 1) * pitch_of(chunk), layers), jnp.float32)],
        ),
        out_shape=[jax.ShapeDtypeStruct((part, x_local, layers), jnp.bfloat16)] * pieces,
        compiler_params=pltpu.CompilerParams(vmem_limit_bytes=VMEM_LIMIT),
        name="forward_y",
    )(me, table, carried)


def inverse_y(me, spectra, rows, modes, step, pressure):
    pieces = len(spectra)
    part, x_local, layers = spectra[0].shape
    chunk = min(CHUNK, x_local)
    table = y_table(rows)
    earlier = [] if pressure is None else [pressure]
    return pl.pallas_call(
        functools.partial(inverse_y_kernel, pieces),
        grid_spec=pltpu.PrefetchScalarGridSpec(
            num_scalar_prefetch=1,
            grid=(x_local // chunk,),
            in_specs=[pl.BlockSpec(table.shape, lambda i, own: (0, 0))]
            + [pl.BlockSpec((part, chunk, layers), lambda i, own: (0, i, 0))] * pieces
            + [pl.BlockSpec(memory_space=pl.ANY)] * len(earlier),
            out_specs=pl.BlockSpec(
                (1, chunk, rows, layers), lambda i, own: (own[0] ^ step, i, 0, 0)
            ),
            scratch_shapes=[pltpu.VMEM(((rows + 1) * pitch_of(chunk), layers), jnp.float32)],
        ),
        out_shape=jax.ShapeDtypeStruct((modes, x_local, rows, layers), jnp.bfloat16),
        input_output_aliases={2 + pieces: 0} if earlier else {},
        compiler_params=pltpu.CompilerParams(vmem_limit_bytes=INVERSE_LIMIT),
        name="inverse_y",
    )(me, table, *spectra, *earlier)


def swap(values, distance):
    return lax.ppermute(
        values, "px", [(k, k ^ distance) for k in range(lax.axis_size("px"))]
    )


def at_layer(k, group, pitch):
    return pl.ds(pl.multiple_of(k * pitch, 8), group)


def eliminate(
    thick_ref, gap_ref, wave_ref, modes, right_side, lower_ref, half_ref, ready=(None,)
):
    layers = thick_ref.shape[0]
    group = wave_ref.shape[1]
    nothing = jnp.zeros(wave_ref.shape, jnp.float32)

    def step(k, carry):
        excess, sums = carry
        thick, inv_gap = thick_ref[k], gap_ref[k]
        spare = wave_ref[...] * thick + excess
        inverse = 1.0 / (spare + inv_gap)
        lower = inverse * inv_gap
        rows = at_layer(k, group, pitch_of(group))
        lower_ref[:, at_layer(k, group, group), :] = lower
        following = []
        for mode in range(modes):
            total = right_side(mode, k, rows) * thick + sums[mode]
            half_ref[mode, :, rows, :] = total * inverse
            following.append(total * lower)
        return (lower * spare, tuple(following))

    carry = (nothing, (nothing,) * modes)
    each = layers // len(ready)
    for at, wait in enumerate(ready):
        if wait is not None:
            wait()
        carry = lax.fori_loop(at * each, (at + 1) * each, step, carry, unroll=4)


def substitute(layers, modes, lower_ref, half_ref, use):
    tiles, all_rows, lanes = lower_ref.shape
    group = all_rows // layers
    nothing = jnp.zeros((tiles, group, lanes), jnp.float32)

    def step(back, values):
        k = layers - 1 - back
        rows = at_layer(k, group, pitch_of(group))
        lower = lower_ref[:, at_layer(k, group, group), :]
        found = []
        for mode in range(modes):
            value = half_ref[mode, :, rows, :] + lower * values[mode]
            use(mode, k, rows, value)
            found.append(value)
        return tuple(found)

    lax.fori_loop(0, layers, step, (nothing,) * modes, unroll=4)


def put_rows(ref, mode, start, group, result):
    layers = result.shape[0]
    for tile in range(ref.shape[1]):
        ref[mode, tile, pl.ds(start, layers, stride=pitch_of(group)), :] = result[
            :, tile * LANES : (tile + 1) * LANES
        ]


def take_rows(ref, mode, start, group, layers):
    return jnp.concatenate(
        [
            ref[mode, tile, pl.ds(start, layers, stride=pitch_of(group)), :].astype(jnp.bfloat16)
            for tile in range(ref.shape[1])
        ],
        axis=1,
    )


def block_ends_kernel(
    count, me_ref, thick_ref, gap_ref, wave_ref, ends_ref, table_ref, strip_table_ref, factor_ref, velocity_ref,
    *refs,
):
    rows_refs, (saved_ref, out_ref, spectrum_ref, lower_ref, half_ref) = refs[:count], refs[count : count + 5]
    end_ref, buffer, arrived, done = refs[count + 5 :]
    part, _, layers = rows_refs[0].shape
    each = min(BATCH, part)
    me = me_ref[0]
    tiles, group, _ = wave_ref.shape
    if group > part:
        spectrum_ref[...] = jnp.zeros_like(spectrum_ref)

    def fetch(at, d):
        some = pl.ds(at * each, each)
        return pltpu.make_async_copy(
            rows_refs[d].at[some], buffer.at[me ^ d, some], arrived.at[at, d]
        )

    for at in range(part // each):
        for d in range(count):
            fetch(at, d).start()

    def transform(b, carry):
        strips = (factor_ref[b] * velocity_ref[...]).astype(jnp.bfloat16)
        left = jnp.concatenate([buffer[c, b] for c in range(count)], axis=0)
        result = contract(left, table_ref[...], 0, 0) + contract(
            strips, strip_table_ref[...], 1, 0
        )
        put_rows(spectrum_ref, 0, b, group, result)
        return carry

    for at in range(part // each):
        for d in range(count):
            fetch(at, d).wait()
        lax.fori_loop(at * each, (at + 1) * each, transform, 0, unroll=2)
    saving = pltpu.make_async_copy(spectrum_ref, saved_ref, done)
    saving.start()
    eliminate(
        thick_ref, gap_ref, wave_ref, 1,
        lambda mode, k, rows: spectrum_ref[mode, :, rows, :], lower_ref, half_ref,
    )

    def use(mode, k, rows, value):
        for end in range(2):
            end_ref[end, :, pl.ds(k, 1), :] = jnp.sum(
                value * ends_ref[end], axis=1, keepdims=True
            )

    substitute(layers, 1, lower_ref, half_ref, use)
    for end in range(2):
        for tile in range(tiles):
            out_ref[tile * LANES : (tile + 1) * LANES, end * layers : (end + 1) * layers] = (
                end_ref[end, tile].T.astype(jnp.bfloat16)
            )
    saving.wait()


def interface_kernel(
    thick_ref, gap_ref, wave_ref, spread_ref, in_ref,
    out_ref, sum_ref, next_ref, spectrum_ref, lower_ref,
):
    group = wave_ref.shape[1]
    layers = thick_ref.shape[0]
    blocks = spread_ref.shape[0] // 2
    modes = in_ref.shape[0]
    here = in_ref.shape[2] // blocks
    if group > here:
        spectrum_ref[...] = jnp.zeros_like(spectrum_ref)
    for mode in range(modes):
        total = jnp.sum(in_ref[mode].astype(jnp.float32), axis=0)
        for end in range(2):
            sum_ref[end * modes + mode, : total.shape[0]] = total[:, end * layers : (end + 1) * layers]

    for a in range(here):
        picked = pl.ds(a, blocks, stride=here)
        for mode in range(modes):
            left = jnp.concatenate(
                [sum_ref[end * modes + mode, picked, :] for end in range(2)], axis=0
            ).astype(jnp.bfloat16)
            put_rows(spectrum_ref, mode, a, group, contract(left, spread_ref[...], 0, 0))
    eliminate(
        thick_ref, gap_ref, wave_ref, modes,
        lambda mode, k, rows: spectrum_ref[mode, :, rows, :], lower_ref, spectrum_ref,
    )

    def use(mode, k, rows, value):
        spectrum_ref[mode, :, rows, :] = value

    substitute(layers, modes, lower_ref, spectrum_ref, use)
    for a in range(here):
        picked = pl.ds(a, blocks, stride=here)
        for mode in range(modes):
            solved = take_rows(spectrum_ref, mode, a, group, layers)
            found = contract(spread_ref[...], solved, 1, 1)
            for end in range(2):
                next_ref[end * modes + mode, picked, :] = found[
                    end * blocks : (end + 1) * blocks
                ]
    inner, every = (blocks - 1) * here, blocks * here
    for mode in range(modes):
        first, last = mode, modes + mode
        next_ref[first, here:every] = next_ref[first, here:every] + sum_ref[last, :inner]
        next_ref[last, :inner] = next_ref[last, :inner] + sum_ref[first, here:every]
    for mode in range(modes):
        for end in range(2):
            outgoing = next_ref[end * modes + mode, :every].astype(jnp.bfloat16)
            for copy in range(out_ref.shape[1]):
                out_ref[mode, copy, :, end * layers : (end + 1) * layers] = outgoing


def block_solve_kernel(
    count, me_ref, thick_ref, gap_ref, wave_ref, ends_ref, table_ref, strip_table_ref, factor_ref, velocity_ref,
    bound_ref,
    saved_ref, *refs,
):
    outs, (mass_ref, lower_ref, spectrum_ref, edge_ref) = refs[:count], refs[count : count + 4]
    outgoing, arrived, sent = refs[count + 4 :]
    part, x_local, layers = outs[0].shape
    each = min(BATCH, part)
    me = me_ref[0]
    tiles, group, _ = wave_ref.shape
    pieces = arrived.shape[0]
    size = layers * pitch_of(group) // pieces
    loads = []
    for at in range(pieces):
        rows = pl.ds(at * size, size)
        loads.append(
            pltpu.make_async_copy(
                saved_ref.at[:, :, rows], spectrum_ref.at[:, :, rows], arrived.at[at]
            )
        )
        loads[-1].start()
    for end in range(2):
        for tile in range(tiles):
            edge_ref[end, tile] = (
                bound_ref[tile * LANES : (tile + 1) * LANES, end * layers : (end + 1) * layers]
                .astype(jnp.float32)
                .T
            )

    def right_side(mode, k, rows):
        total = spectrum_ref[mode, :, rows, :]
        for end in range(2):
            total = total + ends_ref[end] * edge_ref[end, :, pl.ds(k, 1), :]
        return total

    eliminate(
        thick_ref, gap_ref, wave_ref, 1, right_side, lower_ref, spectrum_ref,
        [load.wait for load in loads],
    )

    def use(mode, k, rows, value):
        spectrum_ref[mode, :, rows, :] = value

    substitute(layers, 1, lower_ref, spectrum_ref, use)

    def send(at, d):
        some = pl.ds(at * each, each)
        return pltpu.make_async_copy(outgoing.at[me ^ d, some], outs[d].at[some], sent.at[at, d])

    def transform(pair, at_strips):
        first = pair * 2
        solved = jnp.concatenate(
            [take_rows(spectrum_ref, 0, first + at, group, layers) for at in range(2)], axis=0
        )
        result = contract(table_ref[...], solved, 1, 1)
        for at in range(2):
            b = first + at
            found = result[:, at * layers : (at + 1) * layers]
            for c in range(count):
                outgoing[c, b] = found[c * x_local : (c + 1) * x_local].astype(jnp.bfloat16)
        found = contract(solved, strip_table_ref[...], 1, 1)
        for at in range(2):
            at_strips += found[at * layers : (at + 1) * layers] * factor_ref[first + at]
        return at_strips

    nothing = jnp.zeros(velocity_ref.shape[1:], jnp.float32)
    at_strips = nothing
    for at in range(part // each):
        at_strips = lax.fori_loop(
            at * each // 2, (at + 1) * each // 2, transform, at_strips, unroll=True
        )
        for d in range(count):
            send(at, d).start()
    for mode in range(velocity_ref.shape[0]):
        mass_ref[mode] = at_strips * velocity_ref[mode]
    for at in range(part // each):
        for d in range(count):
            send(at, d).wait()


def shards(carried, velocity, strip_column, thick):
    modes, x_local, y_local, layers = carried.shape
    count_px = lax.axis_size("px")
    count_py = lax.axis_size("py")
    index_px = lax.axis_index("px")
    index_py = lax.axis_index("py")
    devices = count_px * count_py
    width_x = x_local * count_px
    width_y = y_local * count_py
    pieces = count_px // modes
    part = y_local // pieces
    own_mode, own_piece = index_px // pieces, index_px % pieces
    group = -(-part // 8) * 8
    here = width_x // devices
    group_a = -(-here // 8) * 8
    strip_count = velocity.shape[1] * devices
    both = ("px", "py")

    code = jnp.stack([strip_column // 65536, strip_column // 256 % 256, strip_column % 256])
    code = jnp.pad(code.T, ((0, 0), (0, layers - 3))).astype(jnp.bfloat16)
    packed = jnp.concatenate([velocity, code[None]], axis=0).transpose(1, 0, 2)
    own = index_px.astype(jnp.int32).reshape(1)
    place = jnp.stack([own_mode, own_piece]).astype(jnp.int32)
    rows = [None] * count_px
    for step in reversed(range(modes)):
        chunks = list(forward_y(place, carried, pieces, step))
        if step == 0:
            packed, chunks[0] = lax.optimization_barrier((packed, chunks[0]))
        for f, chunk in enumerate(chunks):
            d = step * pieces + f
            rows[d] = swap(chunk, d) if d else chunk
    packed = jnp.broadcast_to(packed[None], (devices,) + packed.shape)
    gathered = lax.all_to_all(packed, both, split_axis=0, concat_axis=0, tiled=True)
    gathered = gathered.reshape(strip_count, modes + 1, layers)
    code = gathered[:, modes, :3].astype(jnp.int32)
    column = code[:, 0] * 65536 + code[:, 1] * 256 + code[:, 2]
    all_velocity = gathered[:, :modes].astype(jnp.float32).transpose(1, 2, 0)
    own_velocity = lax.dynamic_index_in_dim(all_velocity, own_mode, 0, False)

    table_x = bf16(sine_table(width_x))
    table_y = jnp.asarray(sine_table(y_local).astype(np.float32))
    local_y = column % width_y - index_py * y_local
    inside = (local_y >= 0) & (local_y < y_local)
    factor = jnp.where(inside[:, None], table_y[jnp.clip(local_y, 0, y_local - 1)], 0.0)
    factor = lax.dynamic_slice_in_dim(factor, own_piece * part, part, axis=1)
    factor = factor.T[:, None, :]
    table_strips = table_x[column // width_y]

    gap = jnp.concatenate([2.0 / (thick[:-1] + thick[1:]), 2.0 / thick[-1:]])
    wave_x = jnp.asarray(wave_numbers(width_x).astype(np.float32))
    wave_y = jnp.asarray(wave_numbers(width_y).astype(np.float32))
    wave_block = jnp.asarray(wave_numbers(y_local).astype(np.float32))
    wave_b = lax.dynamic_slice_in_dim(wave_block, own_piece * part, part)
    wave_b = jnp.pad(wave_b, (0, group - part))[:, None] + wave_x.reshape(-1, 1, LANES)
    wave_a = lax.dynamic_slice_in_dim(wave_x, (index_px * count_py + index_py) * here, here)
    wave_a = jnp.pad(wave_a, (0, group_a - here))[:, None] + wave_y.reshape(-1, 1, LANES)
    ends = lax.dynamic_slice_in_dim(table_y[:, (0, y_local - 1)], own_piece * part, part)
    ends = jnp.pad(ends.T, ((0, 0), (0, group - part)))[:, :, None]
    ends = jnp.broadcast_to(ends, (2, group, LANES))

    block_index = np.arange(count_py)
    full = sine_table(width_y)
    not_first = (block_index > 0)[:, None]
    not_last = (block_index < count_py - 1)[:, None]
    before = np.maximum(block_index * y_local - 1, 0)
    after = np.minimum((block_index + 1) * y_local, width_y - 1)
    spread = np.concatenate([full[before] * not_first, full[after] * not_last])

    params = pltpu.CompilerParams(vmem_limit_bytes=VMEM_LIMIT)
    vmem = pl.BlockSpec(memory_space=VMEM)
    smem = pl.BlockSpec(memory_space=SMEM)
    anywhere = pl.BlockSpec(memory_space=pl.ANY)
    float32 = jnp.float32
    tiles_x, tiles_y = width_x // LANES, width_y // LANES

    spectrum, block_ends = pl.pallas_call(
        functools.partial(block_ends_kernel, count_px),
        in_specs=[smem] * 3 + [vmem] * 6 + [anywhere] * count_px,
        out_specs=[anywhere, vmem],
        out_shape=[
            jax.ShapeDtypeStruct((1, tiles_x, (layers + 1) * pitch_of(group), LANES), float32),
            jax.ShapeDtypeStruct((width_x, 2 * layers), jnp.bfloat16),
        ],
        scratch_shapes=[
            pltpu.VMEM((1, tiles_x, (layers + 1) * pitch_of(group), LANES), float32),
            pltpu.VMEM((tiles_x, layers * group, LANES), float32),
            pltpu.VMEM((1, tiles_x, (layers + 1) * pitch_of(group), LANES), float32),
            pltpu.VMEM((2, tiles_x, layers, LANES), float32),
            pltpu.VMEM((count_px, part, x_local, layers), jnp.bfloat16),
            pltpu.SemaphoreType.DMA((part // min(BATCH, part), count_px)),
            pltpu.SemaphoreType.DMA(()),
        ],
        compiler_params=params,
        name="block_ends",
    )(own, thick, gap, wave_b, ends, table_x, table_strips, factor, own_velocity, *rows)

    arrived = lax.all_to_all(block_ends, both, split_axis=0, concat_axis=0, tiled=True)
    outgoing = pl.pallas_call(
        interface_kernel,
        in_specs=[smem, smem] + [vmem] * 3,
        out_specs=vmem,
        out_shape=jax.ShapeDtypeStruct(
            (modes, pieces, count_py * here, 2 * layers), jnp.bfloat16
        ),
        scratch_shapes=[
            pltpu.VMEM((2 * modes, (count_py + 1) * here, layers), float32),
            pltpu.VMEM((2 * modes, (count_py + 1) * here, layers), float32),
            pltpu.VMEM((modes, tiles_y, (layers + 1) * pitch_of(group_a), LANES), float32),
            pltpu.VMEM((tiles_y, layers * group_a, LANES), float32),
        ],
        compiler_params=pltpu.CompilerParams(vmem_limit_bytes=24 * 1024 * 1024),
        name="interface",
    )(
        thick, gap, wave_a, bf16(spread),
        arrived.reshape(modes, pieces, count_py * here, 2 * layers),
    )
    bounds = lax.all_to_all(
        outgoing.reshape(width_x, 2 * layers), both, split_axis=0, concat_axis=0, tiled=True
    )

    *returned, mass = pl.pallas_call(
        functools.partial(block_solve_kernel, count_px),
        in_specs=[smem] * 3 + [vmem] * 7 + [anywhere],
        out_specs=[anywhere] * count_px + [vmem],
        out_shape=[jax.ShapeDtypeStruct((part, x_local, layers), jnp.bfloat16)] * count_px
        + [
            jax.ShapeDtypeStruct((modes, layers, strip_count), float32),
        ],
        scratch_shapes=[
            pltpu.VMEM((tiles_x, layers * group, LANES), float32),
            pltpu.VMEM((1, tiles_x, (layers + 1) * pitch_of(group), LANES), float32),
            pltpu.VMEM((2, tiles_x, layers, LANES), float32),
            pltpu.VMEM((count_px, part, x_local, layers), jnp.bfloat16),
            pltpu.SemaphoreType.DMA((8,)),
            pltpu.SemaphoreType.DMA((part // min(BATCH, part), count_px)),
        ],
        compiler_params=params,
        name="block_solve",
    )(
        own, thick, gap, wave_b, ends, table_x, table_strips, factor, all_velocity, bounds,
        spectrum,
    )
    back = [swap(chunk, d) if d else chunk for d, chunk in enumerate(returned)]
    own_row = (jnp.arange(modes) == own_mode)[:, None]
    local_mass = jnp.sum(mass * thick[None, :, None], axis=(1, 2))
    local_mass = jnp.where(own_row, local_mass[None, :], 0.0)
    local_mass = lax.psum(local_mass, "py")
    pressure = None
    for step in range(modes):
        chunks = back[step * pieces : (step + 1) * pieces]
        pressure = inverse_y(place, chunks, y_local, modes, step, pressure)
        if step == 0:
            pressure, local_mass = lax.optimization_barrier((pressure, local_mass))
            every_mass = lax.all_gather(local_mass, "px", axis=0, tiled=False)
    added_mass = jnp.sum(every_mass, axis=0) / (strip_count * layers)
    return (pressure, added_mass)


def solution(mesh):
    return jax.shard_map(
        shards,
        mesh=mesh,
        in_specs=(P(None, "px", "py", None), P(None, ("px", "py"), None), P(("px", "py")), P()),
        out_specs=(P(None, "px", "py", None), P()),
        check_vma=False,
    )
```

```python
import functools
import math

import jax
import jax.numpy as jnp
import ml_dtypes
import numpy as np
from jax import lax
from jax.experimental import pallas as pl
from jax.experimental.pallas import tpu as pltpu
from jax.sharding import PartitionSpec as P

VMEM_LIMIT = 58 * 1024 * 1024
VMEM = pltpu.MemorySpace.VMEM
SMEM = pltpu.MemorySpace.SMEM
LANES = 128
INVERSE_LIMIT = 16 * 1024 * 1024
CHUNK = 64
BATCH = 8


def sine_table(length):
    steps = np.arange(1, length + 1)
    product = steps[:, None] * steps[None, :] % (2 * (length + 1))
    return math.sqrt(2.0 / (length + 1)) * np.sin(product * (math.pi / (length + 1)))


def wave_numbers(length):
    return 4.0 * np.sin(np.arange(1, length + 1) * (math.pi / (2 * (length + 1)))) ** 2


def bf16(table):
    return jnp.asarray(table.astype(ml_dtypes.bfloat16))


def contract(left, right, left_dim, right_dim):
    return lax.dot_general(
        left, right, (((left_dim,), (right_dim,)), ((), ())), preferred_element_type=jnp.float32
    )


def pitch_of(group):
    return group if group // 8 % 2 else group + 8


def forward_y_kernel(me_ref, table_ref, grid_ref, *refs):
    outs, scratch = refs[:-1], refs[-1]
    _, x_chunk, rows, layers = grid_ref.shape
    part = outs[0].shape[0]
    group = table_ref.shape[0] // rows
    pitch = pitch_of(x_chunk)
    for start in range(0, x_chunk, group):
        block = grid_ref[0, start : start + group].reshape(group * rows, layers)
        result = contract(table_ref[...], block, 1, 0)
        for at in range(group):
            scratch[pl.ds(start + at, rows, stride=pitch), :] = result[
                at * rows : (at + 1) * rows
            ]
    for f, out in enumerate(outs):
        first = (me_ref[1] ^ f) * part
        for b in range(part):
            begin = pl.multiple_of((first + b) * pitch, 8)
            out[b] = scratch[pl.ds(begin, x_chunk), :].astype(jnp.bfloat16)


def inverse_y_kernel(pieces, me_ref, table_ref, *refs):
    ins, out_ref, scratch = refs[:pieces], refs[-2], refs[-1]
    _, x_chunk, rows, layers = out_ref.shape
    part = ins[0].shape[0]
    group = table_ref.shape[0] // rows
    pitch = pitch_of(x_chunk)
    for f, value in enumerate(ins):
        first = (me_ref[1] ^ f) * part
        for b in range(part):
            begin = pl.multiple_of((first + b) * pitch, 8)
            scratch[pl.ds(begin, x_chunk), :] = value[b].astype(jnp.float32)
    for start in range(0, x_chunk, group):
        block = jnp.concatenate(
            [scratch[pl.ds(start + at, rows, stride=pitch), :] for at in range(group)], axis=0
        ).astype(jnp.bfloat16)
        result = contract(table_ref[...], block, 1, 0)
        out_ref[0, start : start + group] = result.reshape(group, rows, layers).astype(
            jnp.bfloat16
        )


def y_table(rows):
    group = max(1, 256 // rows)
    return bf16(np.kron(np.eye(group), sine_table(rows)))


def forward_y(me, carried, pieces, step):
    modes, x_local, rows, layers = carried.shape
    chunk = min(CHUNK, x_local)
    part = rows // pieces
    table = y_table(rows)
    return pl.pallas_call(
        forward_y_kernel,
        grid_spec=pltpu.PrefetchScalarGridSpec(
            num_scalar_prefetch=1,
            grid=(x_local // chunk,),
            in_specs=[
                pl.BlockSpec(table.shape, lambda i, own: (0, 0)),
                pl.BlockSpec((1, chunk, rows, layers), lambda i, own: (own[0] ^ step, i, 0, 0)),
            ],
            out_specs=[pl.BlockSpec((part, chunk, layers), lambda i, own: (0, i, 0))] * pieces,
            scratch_shapes=[pltpu.VMEM(((rows + 1) * pitch_of(chunk), layers), jnp.float32)],
        ),
        out_shape=[jax.ShapeDtypeStruct((part, x_local, layers), jnp.bfloat16)] * pieces,
        compiler_params=pltpu.CompilerParams(vmem_limit_bytes=VMEM_LIMIT),
        name="forward_y",
    )(me, table, carried)


def inverse_y(me, spectra, rows, modes, step, pressure):
    pieces = len(spectra)
    part, x_local, layers = spectra[0].shape
    chunk = min(CHUNK, x_local)
    table = y_table(rows)
    earlier = [] if pressure is None else [pressure]
    return pl.pallas_call(
        functools.partial(inverse_y_kernel, pieces),
        grid_spec=pltpu.PrefetchScalarGridSpec(
            num_scalar_prefetch=1,
            grid=(x_local // chunk,),
            in_specs=[pl.BlockSpec(table.shape, lambda i, own: (0, 0))]
            + [pl.BlockSpec((part, chunk, layers), lambda i, own: (0, i, 0))] * pieces
            + [pl.BlockSpec(memory_space=pl.ANY)] * len(earlier),
            out_specs=pl.BlockSpec(
                (1, chunk, rows, layers), lambda i, own: (own[0] ^ step, i, 0, 0)
            ),
            scratch_shapes=[pltpu.VMEM(((rows + 1) * pitch_of(chunk), layers), jnp.float32)],
        ),
        out_shape=jax.ShapeDtypeStruct((modes, x_local, rows, layers), jnp.bfloat16),
        input_output_aliases={2 + pieces: 0} if earlier else {},
        compiler_params=pltpu.CompilerParams(vmem_limit_bytes=INVERSE_LIMIT),
        name="inverse_y",
    )(me, table, *spectra, *earlier)


def swap(values, distance):
    return lax.ppermute(
        values, "px", [(k, k ^ distance) for k in range(lax.axis_size("px"))]
    )


def at_layer(k, group, pitch):
    return pl.ds(pl.multiple_of(k * pitch, 8), group)


def eliminate(
    thick_ref, gap_ref, wave_ref, modes, right_side, lower_ref, half_ref, ready=(None,)
):
    layers = thick_ref.shape[0]
    group = wave_ref.shape[1]
    nothing = jnp.zeros(wave_ref.shape, jnp.float32)

    def step(k, carry):
        excess, sums = carry
        thick, inv_gap = thick_ref[k], gap_ref[k]
        spare = wave_ref[...] * thick + excess
        inverse = 1.0 / (spare + inv_gap)
        lower = inverse * inv_gap
        rows = at_layer(k, group, pitch_of(group))
        lower_ref[:, at_layer(k, group, group), :] = lower
        following = []
        for mode in range(modes):
            total = right_side(mode, k, rows) * thick + sums[mode]
            half_ref[mode, :, rows, :] = total * inverse
            following.append(total * lower)
        return (lower * spare, tuple(following))

    carry = (nothing, (nothing,) * modes)
    each = layers // len(ready)
    for at, wait in enumerate(ready):
        if wait is not None:
            wait()
        carry = lax.fori_loop(at * each, (at + 1) * each, step, carry, unroll=4)


def substitute(layers, modes, lower_ref, half_ref, use):
    tiles, all_rows, lanes = lower_ref.shape
    group = all_rows // layers
    nothing = jnp.zeros((tiles, group, lanes), jnp.float32)

    def step(back, values):
        k = layers - 1 - back
        rows = at_layer(k, group, pitch_of(group))
        lower = lower_ref[:, at_layer(k, group, group), :]
        found = []
        for mode in range(modes):
            value = half_ref[mode, :, rows, :] + lower * values[mode]
            use(mode, k, rows, value)
            found.append(value)
        return tuple(found)

    lax.fori_loop(0, layers, step, (nothing,) * modes, unroll=4)


def put_rows(ref, mode, start, group, result):
    layers = result.shape[0]
    for tile in range(ref.shape[1]):
        ref[mode, tile, pl.ds(start, layers, stride=pitch_of(group)), :] = result[
            :, tile * LANES : (tile + 1) * LANES
        ]


def take_rows(ref, mode, start, group, layers):
    return jnp.concatenate(
        [
            ref[mode, tile, pl.ds(start, layers, stride=pitch_of(group)), :].astype(jnp.bfloat16)
            for tile in range(ref.shape[1])
        ],
        axis=1,
    )


def block_ends_kernel(
    count, me_ref, thick_ref, gap_ref, wave_ref, ends_ref, table_ref, strip_table_ref, factor_ref, velocity_ref,
    *refs,
):
    rows_refs, (saved_ref, out_ref, spectrum_ref, lower_ref, half_ref) = refs[:count], refs[count : count + 5]
    end_ref, buffer, arrived, done = refs[count + 5 :]
    part, _, layers = rows_refs[0].shape
    each = min(BATCH, part)
    me = me_ref[0]
    tiles, group, _ = wave_ref.shape
    if group > part:
        spectrum_ref[...] = jnp.zeros_like(spectrum_ref)

    def fetch(at, d):
        some = pl.ds(at * each, each)
        return pltpu.make_async_copy(
            rows_refs[d].at[some], buffer.at[me ^ d, some], arrived.at[at, d]
        )

    for at in range(part // each):
        for d in range(count):
            fetch(at, d).start()

    def transform(b, carry):
        strips = (factor_ref[b] * velocity_ref[...]).astype(jnp.bfloat16)
        left = jnp.concatenate([buffer[c, b] for c in range(count)], axis=0)
        result = contract(left, table_ref[...], 0, 0) + contract(
            strips, strip_table_ref[...], 1, 0
        )
        put_rows(spectrum_ref, 0, b, group, result)
        return carry

    for at in range(part // each):
        for d in range(count):
            fetch(at, d).wait()
        lax.fori_loop(at * each, (at + 1) * each, transform, 0, unroll=4)
    saving = pltpu.make_async_copy(spectrum_ref, saved_ref, done)
    saving.start()
    eliminate(
        thick_ref, gap_ref, wave_ref, 1,
        lambda mode, k, rows: spectrum_ref[mode, :, rows, :], lower_ref, half_ref,
    )

    def use(mode, k, rows, value):
        for end in range(2):
            end_ref[end, :, pl.ds(k, 1), :] = jnp.sum(
                value * ends_ref[end], axis=1, keepdims=True
            )

    substitute(layers, 1, lower_ref, half_ref, use)
    for end in range(2):
        for tile in range(tiles):
            out_ref[tile * LANES : (tile + 1) * LANES, end * layers : (end + 1) * layers] = (
                end_ref[end, tile].T.astype(jnp.bfloat16)
            )
    saving.wait()


def interface_kernel(
    thick_ref, gap_ref, wave_ref, spread_ref, in_ref,
    out_ref, sum_ref, next_ref, spectrum_ref, lower_ref,
):
    group = wave_ref.shape[1]
    layers = thick_ref.shape[0]
    blocks = spread_ref.shape[0] // 2
    modes = in_ref.shape[0]
    here = in_ref.shape[2] // blocks
    if group > here:
        spectrum_ref[...] = jnp.zeros_like(spectrum_ref)
    for mode in range(modes):
        total = jnp.sum(in_ref[mode].astype(jnp.float32), axis=0)
        for end in range(2):
            sum_ref[end * modes + mode, : total.shape[0]] = total[:, end * layers : (end + 1) * layers]

    for a in range(here):
        picked = pl.ds(a, blocks, stride=here)
        for mode in range(modes):
            left = jnp.concatenate(
                [sum_ref[end * modes + mode, picked, :] for end in range(2)], axis=0
            ).astype(jnp.bfloat16)
            put_rows(spectrum_ref, mode, a, group, contract(left, spread_ref[...], 0, 0))
    eliminate(
        thick_ref, gap_ref, wave_ref, modes,
        lambda mode, k, rows: spectrum_ref[mode, :, rows, :], lower_ref, spectrum_ref,
    )

    def use(mode, k, rows, value):
        spectrum_ref[mode, :, rows, :] = value

    substitute(layers, modes, lower_ref, spectrum_ref, use)
    for a in range(here):
        picked = pl.ds(a, blocks, stride=here)
        for mode in range(modes):
            solved = take_rows(spectrum_ref, mode, a, group, layers)
            found = contract(spread_ref[...], solved, 1, 1)
            for end in range(2):
                next_ref[end * modes + mode, picked, :] = found[
                    end * blocks : (end + 1) * blocks
                ]
    inner, every = (blocks - 1) * here, blocks * here
    for mode in range(modes):
        first, last = mode, modes + mode
        next_ref[first, here:every] = next_ref[first, here:every] + sum_ref[last, :inner]
        next_ref[last, :inner] = next_ref[last, :inner] + sum_ref[first, here:every]
    for mode in range(modes):
        for end in range(2):
            outgoing = next_ref[end * modes + mode, :every].astype(jnp.bfloat16)
            for copy in range(out_ref.shape[1]):
                out_ref[mode, copy, :, end * layers : (end + 1) * layers] = outgoing


def block_solve_kernel(
    count, me_ref, thick_ref, gap_ref, wave_ref, ends_ref, table_ref, strip_table_ref, factor_ref, velocity_ref,
    bound_ref,
    saved_ref, *refs,
):
    outs, (mass_ref, lower_ref, spectrum_ref, edge_ref) = refs[:count], refs[count : count + 4]
    outgoing, arrived, sent = refs[count + 4 :]
    part, x_local, layers = outs[0].shape
    each = min(BATCH, part)
    me = me_ref[0]
    tiles, group, _ = wave_ref.shape
    pieces = arrived.shape[0]
    size = layers * pitch_of(group) // pieces
    loads = []
    for at in range(pieces):
        rows = pl.ds(at * size, size)
        loads.append(
            pltpu.make_async_copy(
                saved_ref.at[:, :, rows], spectrum_ref.at[:, :, rows], arrived.at[at]
            )
        )
        loads[-1].start()
    for end in range(2):
        for tile in range(tiles):
            edge_ref[end, tile] = (
                bound_ref[tile * LANES : (tile + 1) * LANES, end * layers : (end + 1) * layers]
                .astype(jnp.float32)
                .T
            )

    def right_side(mode, k, rows):
        total = spectrum_ref[mode, :, rows, :]
        for end in range(2):
            total = total + ends_ref[end] * edge_ref[end, :, pl.ds(k, 1), :]
        return total

    eliminate(
        thick_ref, gap_ref, wave_ref, 1, right_side, lower_ref, spectrum_ref,
        [load.wait for load in loads],
    )

    def use(mode, k, rows, value):
        spectrum_ref[mode, :, rows, :] = value

    substitute(layers, 1, lower_ref, spectrum_ref, use)

    def send(at, d):
        some = pl.ds(at * each, each)
        return pltpu.make_async_copy(outgoing.at[me ^ d, some], outs[d].at[some], sent.at[at, d])

    def transform(pair, at_strips):
        first = pair * 2
        solved = jnp.concatenate(
            [take_rows(spectrum_ref, 0, first + at, group, layers) for at in range(2)], axis=0
        )
        result = contract(table_ref[...], solved, 1, 1)
        for at in range(2):
            b = first + at
            found = result[:, at * layers : (at + 1) * layers]
            for c in range(count):
                outgoing[c, b] = found[c * x_local : (c + 1) * x_local].astype(jnp.bfloat16)
        found = contract(solved, strip_table_ref[...], 1, 1)
        for at in range(2):
            at_strips += found[at * layers : (at + 1) * layers] * factor_ref[first + at]
        return at_strips

    nothing = jnp.zeros(velocity_ref.shape[1:], jnp.float32)
    at_strips = nothing
    for at in range(part // each):
        at_strips = lax.fori_loop(
            at * each // 2, (at + 1) * each // 2, transform, at_strips, unroll=True
        )
        for d in range(count):
            send(at, d).start()
    for mode in range(velocity_ref.shape[0]):
        mass_ref[mode] = at_strips * velocity_ref[mode]
    for at in range(part // each):
        for d in range(count):
            send(at, d).wait()


def shards(carried, velocity, strip_column, thick):
    modes, x_local, y_local, layers = carried.shape
    count_px = lax.axis_size("px")
    count_py = lax.axis_size("py")
    index_px = lax.axis_index("px")
    index_py = lax.axis_index("py")
    devices = count_px * count_py
    width_x = x_local * count_px
    width_y = y_local * count_py
    pieces = count_px // modes
    part = y_local // pieces
    own_mode, own_piece = index_px // pieces, index_px % pieces
    group = -(-part // 8) * 8
    here = width_x // devices
    group_a = -(-here // 8) * 8
    strip_count = velocity.shape[1] * devices
    both = ("px", "py")

    code = jnp.stack([strip_column // 65536, strip_column // 256 % 256, strip_column % 256])
    code = jnp.pad(code.T, ((0, 0), (0, layers - 3))).astype(jnp.bfloat16)
    packed = jnp.concatenate([velocity, code[None]], axis=0).transpose(1, 0, 2)
    own = index_px.astype(jnp.int32).reshape(1)
    place = jnp.stack([own_mode, own_piece]).astype(jnp.int32)
    rows = [None] * count_px
    for step in reversed(range(modes)):
        chunks = list(forward_y(place, carried, pieces, step))
        if step == 0:
            packed, chunks[0] = lax.optimization_barrier((packed, chunks[0]))
        for f, chunk in enumerate(chunks):
            d = step * pieces + f
            rows[d] = swap(chunk, d) if d else chunk
    packed = jnp.broadcast_to(packed[None], (devices,) + packed.shape)
    gathered = lax.all_to_all(packed, both, split_axis=0, concat_axis=0, tiled=True)
    gathered = gathered.reshape(strip_count, modes + 1, layers)
    code = gathered[:, modes, :3].astype(jnp.int32)
    column = code[:, 0] * 65536 + code[:, 1] * 256 + code[:, 2]
    all_velocity = gathered[:, :modes].astype(jnp.float32).transpose(1, 2, 0)
    own_velocity = lax.dynamic_index_in_dim(all_velocity, own_mode, 0, False)

    table_x = bf16(sine_table(width_x))
    table_y = jnp.asarray(sine_table(y_local).astype(np.float32))
    local_y = column % width_y - index_py * y_local
    inside = (local_y >= 0) & (local_y < y_local)
    factor = jnp.where(inside[:, None], table_y[jnp.clip(local_y, 0, y_local - 1)], 0.0)
    factor = lax.dynamic_slice_in_dim(factor, own_piece * part, part, axis=1)
    factor = factor.T[:, None, :]
    table_strips = table_x[column // width_y]

    gap = jnp.concatenate([2.0 / (thick[:-1] + thick[1:]), 2.0 / thick[-1:]])
    wave_x = jnp.asarray(wave_numbers(width_x).astype(np.float32))
    wave_y = jnp.asarray(wave_numbers(width_y).astype(np.float32))
    wave_block = jnp.asarray(wave_numbers(y_local).astype(np.float32))
    wave_b = lax.dynamic_slice_in_dim(wave_block, own_piece * part, part)
    wave_b = jnp.pad(wave_b, (0, group - part))[:, None] + wave_x.reshape(-1, 1, LANES)
    wave_a = lax.dynamic_slice_in_dim(wave_x, (index_px * count_py + index_py) * here, here)
    wave_a = jnp.pad(wave_a, (0, group_a - here))[:, None] + wave_y.reshape(-1, 1, LANES)
    ends = lax.dynamic_slice_in_dim(table_y[:, (0, y_local - 1)], own_piece * part, part)
    ends = jnp.pad(ends.T, ((0, 0), (0, group - part)))[:, :, None]
    ends = jnp.broadcast_to(ends, (2, group, LANES))

    block_index = np.arange(count_py)
    full = sine_table(width_y)
    not_first = (block_index > 0)[:, None]
    not_last = (block_index < count_py - 1)[:, None]
    before = np.maximum(block_index * y_local - 1, 0)
    after = np.minimum((block_index + 1) * y_local, width_y - 1)
    spread = np.concatenate([full[before] * not_first, full[after] * not_last])

    params = pltpu.CompilerParams(vmem_limit_bytes=VMEM_LIMIT)
    vmem = pl.BlockSpec(memory_space=VMEM)
    smem = pl.BlockSpec(memory_space=SMEM)
    anywhere = pl.BlockSpec(memory_space=pl.ANY)
    float32 = jnp.float32
    tiles_x, tiles_y = width_x // LANES, width_y // LANES

    spectrum, block_ends = pl.pallas_call(
        functools.partial(block_ends_kernel, count_px),
        in_specs=[smem] * 3 + [vmem] * 6 + [anywhere] * count_px,
        out_specs=[anywhere, vmem],
        out_shape=[
            jax.ShapeDtypeStruct((1, tiles_x, (layers + 1) * pitch_of(group), LANES), float32),
            jax.ShapeDtypeStruct((width_x, 2 * layers), jnp.bfloat16),
        ],
        scratch_shapes=[
            pltpu.VMEM((1, tiles_x, (layers + 1) * pitch_of(group), LANES), float32),
            pltpu.VMEM((tiles_x, layers * group, LANES), float32),
            pltpu.VMEM((1, tiles_x, (layers + 1) * pitch_of(group), LANES), float32),
            pltpu.VMEM((2, tiles_x, layers, LANES), float32),
            pltpu.VMEM((count_px, part, x_local, layers), jnp.bfloat16),
            pltpu.SemaphoreType.DMA((part // min(BATCH, part), count_px)),
            pltpu.SemaphoreType.DMA(()),
        ],
        compiler_params=params,
        name="block_ends",
    )(own, thick, gap, wave_b, ends, table_x, table_strips, factor, own_velocity, *rows)

    arrived = lax.all_to_all(block_ends, both, split_axis=0, concat_axis=0, tiled=True)
    outgoing = pl.pallas_call(
        interface_kernel,
        in_specs=[smem, smem] + [vmem] * 3,
        out_specs=vmem,
        out_shape=jax.ShapeDtypeStruct(
            (modes, pieces, count_py * here, 2 * layers), jnp.bfloat16
        ),
        scratch_shapes=[
            pltpu.VMEM((2 * modes, (count_py + 1) * here, layers), float32),
            pltpu.VMEM((2 * modes, (count_py + 1) * here, layers), float32),
            pltpu.VMEM((modes, tiles_y, (layers + 1) * pitch_of(group_a), LANES), float32),
            pltpu.VMEM((tiles_y, layers * group_a, LANES), float32),
        ],
        compiler_params=pltpu.CompilerParams(vmem_limit_bytes=24 * 1024 * 1024),
        name="interface",
    )(
        thick, gap, wave_a, bf16(spread),
        arrived.reshape(modes, pieces, count_py * here, 2 * layers),
    )
    bounds = lax.all_to_all(
        outgoing.reshape(width_x, 2 * layers), both, split_axis=0, concat_axis=0, tiled=True
    )

    *returned, mass = pl.pallas_call(
        functools.partial(block_solve_kernel, count_px),
        in_specs=[smem] * 3 + [vmem] * 7 + [anywhere],
        out_specs=[anywhere] * count_px + [vmem],
        out_shape=[jax.ShapeDtypeStruct((part, x_local, layers), jnp.bfloat16)] * count_px
        + [
            jax.ShapeDtypeStruct((modes, layers, strip_count), float32),
        ],
        scratch_shapes=[
            pltpu.VMEM((tiles_x, layers * group, LANES), float32),
            pltpu.VMEM((1, tiles_x, (layers + 1) * pitch_of(group), LANES), float32),
            pltpu.VMEM((2, tiles_x, layers, LANES), float32),
            pltpu.VMEM((count_px, part, x_local, layers), jnp.bfloat16),
            pltpu.SemaphoreType.DMA((8,)),
            pltpu.SemaphoreType.DMA((part // min(BATCH, part), count_px)),
        ],
        compiler_params=params,
        name="block_solve",
    )(
        own, thick, gap, wave_b, ends, table_x, table_strips, factor, all_velocity, bounds,
        spectrum,
    )
    back = [swap(chunk, d) if d else chunk for d, chunk in enumerate(returned)]
    own_row = (jnp.arange(modes) == own_mode)[:, None]
    local_mass = jnp.sum(mass * thick[None, :, None], axis=(1, 2))
    local_mass = jnp.where(own_row, local_mass[None, :], 0.0)
    local_mass = lax.psum(local_mass, "py")
    pressure = None
    for step in range(modes):
        chunks = back[step * pieces : (step + 1) * pieces]
        pressure = inverse_y(place, chunks, y_local, modes, step, pressure)
        if step == 0:
            pressure, local_mass = lax.optimization_barrier((pressure, local_mass))
            every_mass = lax.all_gather(local_mass, "px", axis=0, tiled=False)
    added_mass = jnp.sum(every_mass, axis=0) / (strip_count * layers)
    return (pressure, added_mass)


def solution(mesh):
    return jax.shard_map(
        shards,
        mesh=mesh,
        in_specs=(P(None, "px", "py", None), P(None, ("px", "py"), None), P(("px", "py")), P()),
        out_specs=(P(None, "px", "py", None), P()),
        check_vma=False,
    )
```
